512 devices in a mesh: dp: 16 (over x, y), tile: 32 (over z, core).
Axes of the slice: x: 4, y: 4, z: 16, core: 2. Of those that a mesh axis runs over, the one named last changes fastest.
Arguments:
- calibration: bfloat16 [2048, 32768], P('dp', 'tile'), may hold values from -72 to 72
- sketch: bfloat16 [32768, 256], P('tile'), may hold values from -6 to 6
- weights: bfloat16 [16384, 32768], P(('dp', 'tile')), may hold values from -6 to 6
- tile_ranks: int32 [16, 32], P('dp', 'tile'), may hold values from 32 to 256
Outputs:
- basis_factor: bfloat16 [16384, 8192], P(('dp', 'tile'))
- coefficients: bfloat16 [4096, 32768], P('dp', 'tile')
The draws below stay inside these ranges and needn't reach their ends.
All inputs are finite; a program needn't handle non-finite values.
Results may differ from the reference program's by a relative error of at most 0.007.
Values may be sent and summed in bfloat16 or wider, within the bound.
No kernel may reach another device: no remote copies, remote signals or barrier semaphores. Data moves between devices by JAX's collectives and lax.ppermute only.
A program may use at most 128 MiB of HBM per device.

```python
import math
import jax
import jax.numpy as jnp
from jax import lax

BS = 1024
RMAX = 256
TOKENS = 2048
OUTB = 16
BLOCKS = 32


def draw_calibration(key, part):
    key = jax.random.fold_in(key, 11)
    keys = jax.random.split(key, 3)
    shape = (TOKENS, BLOCKS * BS)
    row_draw = jax.random.uniform(keys[0], (TOKENS, 1), jnp.float32)
    col_draw = jax.random.uniform(keys[1], (1, BLOCKS * BS), jnp.float32)
    ramp = jnp.arange(TOKENS, dtype=jnp.float32)[:, None] / TOKENS
    row_scale = jnp.exp(math.log(0.5) + row_draw * math.log(4.0)) * jnp.exp(ramp * math.log(3.0))
    col_scale = jnp.exp(math.log(0.3) + col_draw * math.log(10.0))
    values = jnp.clip(jax.random.normal(keys[2], shape, jnp.float32), -4.0, 4.0)
    return (values * row_scale * col_scale).astype(jnp.bfloat16)


def draw_tile_ranks(key, part):
    key = jax.random.fold_in(key, 23)
    keys = jax.random.split(key, 3)
    count = OUTB * BLOCKS
    flat = jax.random.randint(keys[0], (count,), RMAX // 8, RMAX + 1, dtype=jnp.int32)
    highest = jax.random.randint(keys[1], (), 0, count, dtype=jnp.int32)
    lowest = (highest + 1 + jax.random.randint(keys[2], (), 0, count - 1, dtype=jnp.int32)) % count
    flat = flat.at[highest].set(RMAX).at[lowest].set(RMAX // 8)
    return flat.reshape(OUTB, BLOCKS).astype(jnp.int32)


def block_levels(own_key, shape, cuts, least, high):
    factor_of = 1.0
    for dim, shards_of in cuts:
        draws = jax.random.uniform(jax.random.fold_in(jax.random.fold_in(own_key, 6), dim), (shards_of,), jnp.float32, least / len(cuts), high / len(cuts))
        factor_of = factor_of * jnp.repeat(jnp.exp(draws), shape[dim] // shards_of).reshape((-1,) + (1,) * (len(shape) - 1 - dim))
    return factor_of


def centred(stream_key, shape, scale, bound, cuts=(), kind=jnp.bfloat16):
    loudness = block_levels(stream_key, shape, cuts, -0.22, 0.18) if cuts else 1.0
    drawn = jax.random.normal(stream_key, shape, jnp.float32) * scale * loudness
    return jnp.minimum(jnp.maximum(drawn, -bound), bound).astype(kind)


def setup_inputs(seed: int = 0) -> dict:
    arg_keys = jax.random.split(jax.random.key(seed), 5)
    return {
        "calibration": draw_calibration(jax.random.fold_in(arg_keys[4], 71), 0),
        "sketch": centred(arg_keys[1], (BLOCKS * BS, RMAX), 1.0, 6.0, ((0, 32),)),
        "weights": centred(arg_keys[2], (OUTB * BS, BLOCKS * BS), 1.0, 6.0, ((0, 512),)),
        "tile_ranks": draw_tile_ranks(jax.random.fold_in(arg_keys[4], 71), 0),
    }


DAMPING = 0.1

def factor(gram):
    width = gram.shape[0]
    mean_diag = jnp.mean(jnp.diagonal(gram))
    held = gram + DAMPING * mean_diag * jnp.eye(width, dtype=jnp.float32)
    return jnp.linalg.cholesky(held)

def compress(tile_block, sketched, tile_rank):
    width = tile_block.shape[0]
    columns = jnp.arange(sketched.shape[1], dtype=jnp.int32)
    kept_cols = columns < tile_rank
    masked = sketched * kept_cols.astype(jnp.bfloat16)
    range_rows = jnp.dot(tile_block.astype(jnp.float32), masked.astype(jnp.float32), preferred_element_type=jnp.float32)
    inner_gram = lax.dot_general(range_rows, range_rows, (((0,), (0,)), ((), ())), precision=lax.Precision.HIGHEST)
    inner_gram = inner_gram + jnp.diag(1.0 - kept_cols.astype(jnp.float32))
    inner_lower = jnp.linalg.cholesky(inner_gram)
    basis_t = jax.scipy.linalg.solve_triangular(inner_lower, range_rows.T, lower=True) * math.sqrt(width)
    basis_bf = basis_t.astype(jnp.bfloat16)
    coeffs = jnp.dot(basis_bf.astype(jnp.float32), tile_block.astype(jnp.float32), preferred_element_type=jnp.float32) / math.sqrt(width)
    return (basis_bf.T, coeffs.astype(jnp.bfloat16))

def reference(calibration, sketch, weights, tile_ranks):

    def block_sketch(block):
        start = (block * BS).astype(jnp.int32)
        cols = lax.dynamic_slice_in_dim(calibration, start, BS, 1)
        gram = jnp.dot(cols.T.astype(jnp.float32), cols.astype(jnp.float32), preferred_element_type=jnp.float32)
        whitener = factor(gram)
        omega_cols = lax.dynamic_slice_in_dim(sketch, start, BS, 0).astype(jnp.float32)
        return jnp.dot(whitener, omega_cols, precision=lax.Precision.HIGHEST).astype(jnp.bfloat16)
    sketched_all = lax.map(block_sketch, jnp.arange(BLOCKS, dtype=jnp.int32))

    def output_row(outer):
        rows = lax.dynamic_slice_in_dim(weights, (outer * BS).astype(jnp.int32), BS, 0)

        def tile_work(block):
            tile_block = lax.dynamic_slice_in_dim(rows, (block * BS).astype(jnp.int32), BS, 1)
            return compress(tile_block, sketched_all[block], tile_ranks[outer, block])
        return lax.map(tile_work, jnp.arange(BLOCKS, dtype=jnp.int32))
    bases, coeffs = lax.map(output_row, jnp.arange(OUTB, dtype=jnp.int32))
    basis_factor = bases.transpose(0, 2, 1, 3).reshape(OUTB * BS, BLOCKS * RMAX)
    coefficients = coeffs.transpose(0, 2, 1, 3).reshape(OUTB * RMAX, BLOCKS * BS)
    return (basis_factor, coefficients)
```

```python
import functools
import math

import jax
import jax.numpy as jnp
from jax import lax
from jax.experimental import pallas as pl
from jax.experimental.pallas import tpu as pltpu
from jax.sharding import PartitionSpec as P

DAMPING = 0.1
NB = 128
STRIP = 8
F32 = jnp.float32
BF16 = jnp.bfloat16

NT = (((1,), (1,)), ((), ()))
NN = (((1,), (0,)), ((), ()))


def dot(a, b, dims):
    return lax.dot_general(a, b, dims, preferred_element_type=F32)


def split2(x):
    hi = x.astype(BF16)
    lo = (x - hi.astype(F32)).astype(BF16)
    return hi, lo


def split3(x):
    hi = x.astype(BF16)
    rest = x - hi.astype(F32)
    mid = rest.astype(BF16)
    lo = (rest - mid.astype(F32)).astype(BF16)
    return hi, mid, lo


def dot3(a, b, dims):
    ah, al = split2(a)
    bh, bl = split2(b)
    return dot(ah, bh, dims) + (dot(ah, bl, dims) + dot(al, bh, dims))


def dot6(a, b, dims):
    ah, am, al = split3(a)
    bh, bm, bl = split3(b)
    small = dot(am, bm, dims) + (dot(ah, bl, dims) + dot(al, bh, dims))
    return dot(ah, bh, dims) + ((dot(ah, bm, dims) + dot(am, bh, dims)) + small)


def recip(x):
    r = pl.reciprocal(x, approx=True)
    r = r * (2.0 - x * r)
    return r * (2.0 - x * r)


def inverse_factor(rows):
    shape = rows[0].shape
    lane = lax.broadcasted_iota(jnp.int32, shape, 1)
    sub = lax.broadcasted_iota(jnp.int32, shape, 0)
    rows = list(rows)
    out = []
    for s in range(len(rows)):
        base = s * STRIP
        strip = rows[s]
        cols = [jnp.broadcast_to(strip[:, base + k : base + k + 1], shape) for k in range(STRIP)]
        a = [
            [jnp.broadcast_to(cols[k][i : i + 1, :], shape) if i >= k else None for k in range(STRIP)]
            for i in range(STRIP)
        ]
        own = (lane >= base) & (lane < base + STRIP)
        held = jnp.where(own, jnp.where(lane - base == sub, 1.0, 0.0), strip)
        y = [jnp.broadcast_to(held[k : k + 1, :], shape) for k in range(STRIP)]
        z = []
        low = [[None] * STRIP for _ in range(STRIP)]
        done = jnp.zeros(shape, F32)
        for k in range(STRIP):
            r = recip(a[k][k])
            for i in range(k + 1, STRIP):
                low[i][k] = a[i][k] * r
            for i in range(k + 1, STRIP):
                for j in range(k + 1, i + 1):
                    a[i][j] = a[i][j] - low[i][k] * a[j][k]
                y[i] = y[i] - low[i][k] * y[k]
            z.append(y[k] * r)
            done = jnp.where(sub == k, y[k] * lax.rsqrt(a[k][k]), done)
        out.append(jnp.where(lane < base + STRIP, done, 0.0))
        if s + 1 == len(rows):
            break
        for k in range(STRIP - 1, -1, -1):
            for i in range(k):
                z[i] = z[i] - low[k][i] * z[k]
        for t in range(s + 1, len(rows)):
            low_t = rows[t]
            total = jnp.where(own, 0.0, low_t)
            for k in range(STRIP - 1, -1, -1):
                total = total - jnp.broadcast_to(low_t[:, base + k : base + k + 1], shape) * z[k]
            rows[t] = total
    return out


def load_strips(ref, index, start):
    return [ref[index, pl.ds(start + s * STRIP, STRIP), :] for s in range(NB // STRIP)]


def turn_kernel(x_ref, out_ref):
    out_ref[...] = x_ref[...].T


def turn(x):
    return pl.pallas_call(
        turn_kernel,
        out_shape=jax.ShapeDtypeStruct((x.shape[1], x.shape[0]), x.dtype),
        in_specs=[pl.BlockSpec(memory_space=pltpu.VMEM)],
        out_specs=pl.BlockSpec(memory_space=pltpu.VMEM),
    )(x)


def whiten_kernel(x_ref, sketch_ref, out_ref, a_ref, hl_ref, rr_ref, rl_ref, acc_ref, inv_ref):
    width = x_ref.shape[1]
    panels = width // NB
    chunks = x_ref.shape[0]
    wide = 2 * NB
    for c in range(panels // 2):
        lo = c * wide
        total = None
        for d in range(0, chunks, 2):
            left = jnp.concatenate([x_ref[d, lo:, :], x_ref[d + 1, lo:, :]], axis=1)
            term = dot(left, left[:wide, :], NT)
            total = term if total is None else total + term
        a_ref[2 * c, lo:, :] = total[:, :NB]
        a_ref[2 * c + 1, lo:, :] = total[:, NB:]

    lane = lax.broadcasted_iota(jnp.int32, (NB, NB), 1)
    sub = lax.broadcasted_iota(jnp.int32, (NB, NB), 0)
    diag = lane == sub
    trace = jnp.zeros((NB, NB), F32)
    for c in range(panels):
        trace = trace + jnp.where(diag, a_ref[c, c * NB : (c + 1) * NB, :], 0.0)
    damp = jnp.sum(trace) * (DAMPING / width)
    for c in range(panels):
        block = a_ref[c, c * NB : (c + 1) * NB, :]
        a_ref[c, c * NB : (c + 1) * NB, :] = jnp.where(diag, block + damp, block)

    hl_ref[...] = jnp.zeros_like(hl_ref)
    rr_ref[...] = jnp.zeros_like(rr_ref)
    rl_ref[...] = jnp.zeros_like(rl_ref)
    acc_ref[...] = jnp.zeros_like(acc_ref)

    tall_row = lax.broadcasted_iota(jnp.int32, (width, NB), 0)
    tall_lane = lax.broadcasted_iota(jnp.int32, (width, NB), 1)

    def sketch_in(p):
        part = sketch_ref[p]
        acc_ref[...] += dot(jnp.concatenate([part, part], axis=1), hl_ref[...], NT)

    def step(p, carry):
        start = pl.multiple_of(p * NB, NB)
        strips = load_strips(a_ref, p, start)
        for c in range(panels // 2):
            lo = c * wide
            both = hl_ref[lo:, :]
            off = dot(both, rr_ref[lo : lo + wide, :], NT) + dot(both[:, :NB], rl_ref[lo : lo + wide, :], NT)
            a_ref[2 * c, lo:, :] -= off[:, :NB]
            a_ref[2 * c + 1, lo:, :] -= off[:, NB:]
        sketch_in(jnp.maximum(p - 1, 0))
        for s, rows in enumerate(inverse_factor(strips)):
            inv_ref[s * STRIP : (s + 1) * STRIP, :] = rows
        ih, il = split2(inv_ref[...])
        ph, plow = split2(a_ref[p])
        panel = dot(jnp.concatenate([ph, plow], axis=1), jnp.concatenate([ih, ih], axis=1), NT) + dot(ph, il, NT)
        panel = jnp.where(tall_row >= tall_lane + start, panel, 0.0)
        hi, lo16 = split2(panel)
        hl_ref[:, :NB] = hi
        hl_ref[:, NB:] = lo16
        right = tall_row >= start + 2 * NB
        hi_r = jnp.where(right, panel, 0.0).astype(BF16)
        rr_ref[:, :NB] = hi_r
        rr_ref[:, NB:] = hi_r
        rl_ref[...] = jnp.where(right, panel - hi.astype(F32), 0.0).astype(BF16)
        nxt = jnp.minimum(p + 1, panels - 1)
        rows_n = pl.ds(pl.multiple_of(nxt * NB, NB), NB)
        near = hl_ref[rows_n, :]
        nh, nl = near[:, :NB], near[:, NB:]
        off = dot(jnp.concatenate([hi, lo16], axis=1), jnp.concatenate([nh, nh], axis=1), NT) + dot(hi, nl, NT)
        a_ref[nxt] = a_ref[nxt] - off
        return carry

    lax.fori_loop(0, panels, step, 0)
    sketch_in(panels - 1)
    out_ref[...] = acc_ref[...].astype(BF16)


def whiten(gathered, sketch_t):
    chunks, width, _ = gathered.shape
    panels, rmax, _ = sketch_t.shape
    return pl.pallas_call(
        whiten_kernel,
        out_shape=jax.ShapeDtypeStruct((rmax, width), BF16),
        in_specs=[pl.BlockSpec(memory_space=pltpu.VMEM)] * 2,
        out_specs=pl.BlockSpec(memory_space=pltpu.VMEM),
        scratch_shapes=[
            pltpu.VMEM((panels, width, NB), F32),
            pltpu.VMEM((width, 2 * NB), BF16),
            pltpu.VMEM((width, 2 * NB), BF16),
            pltpu.VMEM((width, NB), BF16),
            pltpu.VMEM((rmax, width), F32),
            pltpu.VMEM((NB, NB), F32),
        ],
        compiler_params=pltpu.CompilerParams(vmem_limit_bytes=40 * 1024 * 1024),
    )(gathered, sketch_t)


def basis_kernel(rank_ref, w_ref, sk_ref, turned_ref, basis_ref, t_ref, d_ref, off_ref, inv_ref):
    width = w_ref.shape[0]
    rmax = sk_ref.shape[0]
    rank = rank_ref[0, 0]
    kept = lax.broadcasted_iota(jnp.int32, sk_ref.shape, 0) < rank
    masked = jnp.where(kept, sk_ref[...].astype(F32), 0.0).astype(BF16)
    rows = dot(masked, w_ref[...], NT)
    inner = dot6(rows, rows, NT)
    sub = lax.broadcasted_iota(jnp.int32, (rmax, rmax), 0)
    lane = lax.broadcasted_iota(jnp.int32, (rmax, rmax), 1)
    inner = inner + jnp.where((sub == lane) & (sub >= rank), 1.0, 0.0)
    t_ref[0] = rows[:NB]
    t_ref[1] = rows[NB:]
    d_ref[0] = inner[:NB, :NB]
    d_ref[1] = inner[NB:, NB:]
    off_ref[...] = inner[NB:, :NB]

    def step(p, carry):
        for s, part in enumerate(inverse_factor(load_strips(d_ref, p, 0))):
            inv_ref[s * STRIP : (s + 1) * STRIP, :] = part
        inv = inv_ref[...]
        base = dot3(inv, t_ref[p], NN)
        low = dot6(off_ref[...], inv, NT)
        d_ref[1] = d_ref[1] - dot6(low, low, NT)
        t_ref[1] = t_ref[1] - dot6(low, base, NN)
        scaled = base * math.sqrt(width)
        turned_ref[p] = scaled.astype(BF16)
        basis_ref[:, pl.ds(pl.multiple_of(p * NB, NB), NB)] = scaled.T.astype(BF16)
        return carry

    lax.fori_loop(0, rmax // NB, step, 0)


def basis_of(rank, tile_block, sketched_t):
    width = tile_block.shape[0]
    rmax = sketched_t.shape[0]
    halves = rmax // NB
    return pl.pallas_call(
        basis_kernel,
        out_shape=(
            jax.ShapeDtypeStruct((halves, NB, width), BF16),
            jax.ShapeDtypeStruct((width, rmax), BF16),
        ),
        in_specs=[
            pl.BlockSpec(memory_space=pltpu.SMEM),
            pl.BlockSpec(memory_space=pltpu.VMEM),
            pl.BlockSpec(memory_space=pltpu.VMEM),
        ],
        out_specs=(pl.BlockSpec(memory_space=pltpu.VMEM),) * 2,
        scratch_shapes=[
            pltpu.VMEM((halves, NB, width), F32),
            pltpu.VMEM((halves, NB, NB), F32),
            pltpu.VMEM((NB, NB), F32),
            pltpu.VMEM((NB, NB), F32),
        ],
        compiler_params=pltpu.CompilerParams(vmem_limit_bytes=40 * 1024 * 1024),
    )(rank, tile_block, sketched_t)


def local(calibration, sketch, weights, tile_ranks):
    width = calibration.shape[1]
    rmax = sketch.shape[1]
    gathered = lax.all_gather(turn(calibration), "dp")
    sketch_t = sketch.reshape(width // NB, NB, rmax).transpose(0, 2, 1)
    tile_block = lax.all_to_all(weights, "tile", split_axis=1, concat_axis=0, tiled=True)
    sketched_t = whiten(gathered, sketch_t)
    turned, basis = basis_of(tile_ranks, tile_block, sketched_t)
    served = lax.all_to_all(basis, "tile", split_axis=0, concat_axis=1, tiled=True)
    coeffs = jnp.dot(turned.reshape(rmax, width), tile_block, preferred_element_type=F32) / math.sqrt(width)
    return (served, coeffs.astype(BF16))


def solution(mesh):
    placed = (P("dp", "tile"), P("tile", None), P(("dp", "tile"), None), P("dp", "tile"))
    return jax.shard_map(
        local,
        mesh=mesh,
        in_specs=placed,
        out_specs=(P(("dp", "tile"), None), P("dp", "tile")),
        check_vma=False,
    )
```

```python
import functools
import math

import jax
import jax.numpy as jnp
from jax import lax
from jax.experimental import pallas as pl
from jax.experimental.pallas import tpu as pltpu
from jax.sharding import PartitionSpec as P

DAMPING = 0.1
NB = 128
STRIP = 8
F32 = jnp.float32
BF16 = jnp.bfloat16

NT = (((1,), (1,)), ((), ()))
NN = (((1,), (0,)), ((), ()))


def dot(a, b, dims):
    return lax.dot_general(a, b, dims, preferred_element_type=F32)


def split2(x):
    hi = x.astype(BF16)
    lo = (x - hi.astype(F32)).astype(BF16)
    return hi, lo


def split3(x):
    hi = x.astype(BF16)
    rest = x - hi.astype(F32)
    mid = rest.astype(BF16)
    lo = (rest - mid.astype(F32)).astype(BF16)
    return hi, mid, lo


def dot3(a, b, dims):
    ah, al = split2(a)
    bh, bl = split2(b)
    return dot(ah, bh, dims) + (dot(ah, bl, dims) + dot(al, bh, dims))


def dot6(a, b, dims):
    ah, am, al = split3(a)
    bh, bm, bl = split3(b)
    small = dot(am, bm, dims) + (dot(ah, bl, dims) + dot(al, bh, dims))
    return dot(ah, bh, dims) + ((dot(ah, bm, dims) + dot(am, bh, dims)) + small)


def recip(x):
    r = pl.reciprocal(x, approx=True)
    r = r * (2.0 - x * r)
    return r * (2.0 - x * r)


def inverse_factor(rows):
    shape = rows[0].shape
    lane = lax.broadcasted_iota(jnp.int32, shape, 1)
    sub = lax.broadcasted_iota(jnp.int32, shape, 0)
    rows = list(rows)
    out = []
    for s in range(len(rows)):
        base = s * STRIP
        strip = rows[s]
        cols = [jnp.broadcast_to(strip[:, base + k : base + k + 1], shape) for k in range(STRIP)]
        a = [
            [jnp.broadcast_to(cols[k][i : i + 1, :], shape) if i >= k else None for k in range(STRIP)]
            for i in range(STRIP)
        ]
        own = (lane >= base) & (lane < base + STRIP)
        held = jnp.where(own, jnp.where(lane - base == sub, 1.0, 0.0), strip)
        y = [jnp.broadcast_to(held[k : k + 1, :], shape) for k in range(STRIP)]
        z = []
        low = [[None] * STRIP for _ in range(STRIP)]
        done = jnp.zeros(shape, F32)
        for k in range(STRIP):
            r = recip(a[k][k])
            for i in range(k + 1, STRIP):
                low[i][k] = a[i][k] * r
            for i in range(k + 1, STRIP):
                for j in range(k + 1, i + 1):
                    a[i][j] = a[i][j] - low[i][k] * a[j][k]
                y[i] = y[i] - low[i][k] * y[k]
            z.append(y[k] * r)
            done = jnp.where(sub == k, y[k] * lax.rsqrt(a[k][k]), done)
        out.append(jnp.where(lane < base + STRIP, done, 0.0))
        if s + 1 == len(rows):
            break
        for k in range(STRIP - 1, -1, -1):
            for i in range(k):
                z[i] = z[i] - low[k][i] * z[k]
        for t in range(s + 1, len(rows)):
            low_t = rows[t]
            total = jnp.where(own, 0.0, low_t)
            for k in range(STRIP - 1, -1, -1):
                total = total - jnp.broadcast_to(low_t[:, base + k : base + k + 1], shape) * z[k]
            rows[t] = total
    return out


def load_strips(ref, index, start):
    return [ref[index, pl.ds(start + s * STRIP, STRIP), :] for s in range(NB // STRIP)]


def turn_kernel(x_ref, out_ref):
    out_ref[...] = x_ref[...].T


def turn(x):
    return pl.pallas_call(
        turn_kernel,
        out_shape=jax.ShapeDtypeStruct((x.shape[1], x.shape[0]), x.dtype),
        in_specs=[pl.BlockSpec(memory_space=pltpu.VMEM)],
        out_specs=pl.BlockSpec(memory_space=pltpu.VMEM),
    )(x)


def neighbour(value, axis, shift, side=4):
    pairs = []
    for x in range(side):
        for y in range(side):
            to = ((x + shift) % side, y) if axis == 0 else (x, (y + shift) % side)
            pairs.append((x * side + y, to[0] * side + to[1]))
    return lax.ppermute(value, "dp", pairs)


def gather_line(value, axis):
    back = neighbour(value, axis, 1)
    ahead = neighbour(value, axis, -1)
    half = value.shape[0] // 2
    far_a = neighbour(back[:half], axis, 1)
    far_b = neighbour(ahead[half:], axis, -1)
    return value, back, ahead, far_a, far_b


def gather_plane(half, axis):
    near, back, ahead, far_a, far_b = gather_line(half, axis)
    line = jnp.stack([near, back, ahead, jnp.concatenate([far_a, far_b], axis=0)])
    return gather_line(line, 1 - axis)


def whiten_kernel(*refs):
    first, second = refs[:5], refs[5:10]
    sketch_ref, out_ref, a_ref, hl_ref, rr_ref, rl_ref, acc_ref, inv_ref = refs[10:]
    half, _ = first[0].shape[1:]
    width = 2 * half
    panels = width // NB
    wide = 2 * NB

    def piece(parts, group, place):
        if group < 3:
            return parts[group][place]
        return parts[3 + place // 2][place % 2]

    def chunk(dx, dy, upper):
        return piece(first, dy, dx) if upper else piece(second, dx, dy)

    for c in range(panels // 2):
        lo = c * wide
        top = bottom = None
        for dx in range(0, 4, 2):
            for dy in range(4):
                low_part = jnp.concatenate([chunk(dx, dy, False), chunk(dx + 1, dy, False)], axis=1)
                if lo < half:
                    high_part = jnp.concatenate([chunk(dx, dy, True), chunk(dx + 1, dy, True)], axis=1)
                    right = high_part[lo : lo + wide, :]
                    term = dot(high_part[lo:, :], right, NT)
                    top = term if top is None else top + term
                    term = dot(low_part, right, NT)
                else:
                    at = lo - half
                    term = dot(low_part[at:, :], low_part[at : at + wide, :], NT)
                bottom = term if bottom is None else bottom + term
        if lo < half:
            a_ref[2 * c, lo:half, :] = top[:, :NB]
            a_ref[2 * c + 1, lo:half, :] = top[:, NB:]
        from_row = max(lo, half)
        a_ref[2 * c, from_row:, :] = bottom[:, :NB]
        a_ref[2 * c + 1, from_row:, :] = bottom[:, NB:]

    lane = lax.broadcasted_iota(jnp.int32, (NB, NB), 1)
    sub = lax.broadcasted_iota(jnp.int32, (NB, NB), 0)
    diag = lane == sub
    trace = jnp.zeros((NB, NB), F32)
    for c in range(panels):
        trace = trace + jnp.where(diag, a_ref[c, c * NB : (c + 1) * NB, :], 0.0)
    damp = jnp.sum(trace) * (DAMPING / width)
    for c in range(panels):
        block = a_ref[c, c * NB : (c + 1) * NB, :]
        a_ref[c, c * NB : (c + 1) * NB, :] = jnp.where(diag, block + damp, block)

    hl_ref[...] = jnp.zeros_like(hl_ref)
    rr_ref[...] = jnp.zeros_like(rr_ref)
    rl_ref[...] = jnp.zeros_like(rl_ref)
    acc_ref[...] = jnp.zeros_like(acc_ref)

    tall_row = lax.broadcasted_iota(jnp.int32, (width, NB), 0)
    tall_lane = lax.broadcasted_iota(jnp.int32, (width, NB), 1)

    def sketch_in(p):
        part = sketch_ref[p]
        acc_ref[...] += dot(jnp.concatenate([part, part], axis=1), hl_ref[...], NT)

    def step(p, carry):
        start = pl.multiple_of(p * NB, NB)
        strips = load_strips(a_ref, p, start)
        for c in range(panels // 2):
            lo = c * wide
            both = hl_ref[lo:, :]
            off = dot(both, rr_ref[lo : lo + wide, :], NT) + dot(both[:, :NB], rl_ref[lo : lo + wide, :], NT)
            a_ref[2 * c, lo:, :] -= off[:, :NB]
            a_ref[2 * c + 1, lo:, :] -= off[:, NB:]
        sketch_in(jnp.maximum(p - 1, 0))
        for s, rows in enumerate(inverse_factor(strips)):
            inv_ref[s * STRIP : (s + 1) * STRIP, :] = rows
        ih, il = split2(inv_ref[...])
        ph, plow = split2(a_ref[p])
        panel = dot(jnp.concatenate([ph, plow], axis=1), jnp.concatenate([ih, ih], axis=1), NT) + dot(ph, il, NT)
        panel = jnp.where(tall_row >= tall_lane + start, panel, 0.0)
        hi, lo16 = split2(panel)
        hl_ref[:, :NB] = hi
        hl_ref[:, NB:] = lo16
        right = tall_row >= start + 2 * NB
        hi_r = jnp.where(right, panel, 0.0).astype(BF16)
        rr_ref[:, :NB] = hi_r
        rr_ref[:, NB:] = hi_r
        rl_ref[...] = jnp.where(right, panel - hi.astype(F32), 0.0).astype(BF16)
        nxt = jnp.minimum(p + 1, panels - 1)
        rows_n = pl.ds(pl.multiple_of(nxt * NB, NB), NB)
        near = hl_ref[rows_n, :]
        nh, nl = near[:, :NB], near[:, NB:]
        off = dot(jnp.concatenate([hi, lo16], axis=1), jnp.concatenate([nh, nh], axis=1), NT) + dot(hi, nl, NT)
        a_ref[nxt] = a_ref[nxt] - off
        return carry

    lax.fori_loop(0, panels, step, 0)
    sketch_in(panels - 1)
    out_ref[...] = acc_ref[...].astype(BF16)


def whiten(parts, sketch_t):
    width = 2 * parts[0].shape[1]
    panels, rmax, _ = sketch_t.shape
    return pl.pallas_call(
        whiten_kernel,
        out_shape=jax.ShapeDtypeStruct((rmax, width), BF16),
        in_specs=[pl.BlockSpec(memory_space=pltpu.VMEM)] * 11,
        out_specs=pl.BlockSpec(memory_space=pltpu.VMEM),
        scratch_shapes=[
            pltpu.VMEM((panels, width, NB), F32),
            pltpu.VMEM((width, 2 * NB), BF16),
            pltpu.VMEM((width, 2 * NB), BF16),
            pltpu.VMEM((width, NB), BF16),
            pltpu.VMEM((rmax, width), F32),
            pltpu.VMEM((NB, NB), F32),
        ],
        compiler_params=pltpu.CompilerParams(vmem_limit_bytes=40 * 1024 * 1024),
    )(*parts, sketch_t)


def basis_kernel(rank_ref, w_ref, sk_ref, turned_ref, basis_ref, t_ref, d_ref, off_ref, inv_ref):
    width = w_ref.shape[0]
    rmax = sk_ref.shape[0]
    rank = rank_ref[0, 0]
    kept = lax.broadcasted_iota(jnp.int32, sk_ref.shape, 0) < rank
    masked = jnp.where(kept, sk_ref[...].astype(F32), 0.0).astype(BF16)
    rows = dot(masked, w_ref[...], NT)
    inner = dot6(rows, rows, NT)
    sub = lax.broadcasted_iota(jnp.int32, (rmax, rmax), 0)
    lane = lax.broadcasted_iota(jnp.int32, (rmax, rmax), 1)
    inner = inner + jnp.where((sub == lane) & (sub >= rank), 1.0, 0.0)
    t_ref[0] = rows[:NB]
    t_ref[1] = rows[NB:]
    d_ref[0] = inner[:NB, :NB]
    d_ref[1] = inner[NB:, NB:]
    off_ref[...] = inner[NB:, :NB]

    def step(p, carry):
        for s, part in enumerate(inverse_factor(load_strips(d_ref, p, 0))):
            inv_ref[s * STRIP : (s + 1) * STRIP, :] = part
        inv = inv_ref[...]
        base = dot3(inv, t_ref[p], NN)
        low = dot6(off_ref[...], inv, NT)
        d_ref[1] = d_ref[1] - dot6(low, low, NT)
        t_ref[1] = t_ref[1] - dot6(low, base, NN)
        scaled = base * math.sqrt(width)
        turned_ref[p] = scaled.astype(BF16)
        basis_ref[:, pl.ds(pl.multiple_of(p * NB, NB), NB)] = scaled.T.astype(BF16)
        return carry

    lax.fori_loop(0, rmax // NB, step, 0)


def basis_of(rank, tile_block, sketched_t):
    width = tile_block.shape[0]
    rmax = sketched_t.shape[0]
    halves = rmax // NB
    return pl.pallas_call(
        basis_kernel,
        out_shape=(
            jax.ShapeDtypeStruct((halves, NB, width), BF16),
            jax.ShapeDtypeStruct((width, rmax), BF16),
        ),
        in_specs=[
            pl.BlockSpec(memory_space=pltpu.SMEM),
            pl.BlockSpec(memory_space=pltpu.VMEM),
            pl.BlockSpec(memory_space=pltpu.VMEM),
        ],
        out_specs=(pl.BlockSpec(memory_space=pltpu.VMEM),) * 2,
        scratch_shapes=[
            pltpu.VMEM((halves, NB, width), F32),
            pltpu.VMEM((halves, NB, NB), F32),
            pltpu.VMEM((NB, NB), F32),
            pltpu.VMEM((NB, NB), F32),
        ],
        compiler_params=pltpu.CompilerParams(vmem_limit_bytes=40 * 1024 * 1024),
    )(rank, tile_block, sketched_t)


def local(calibration, sketch, weights, tile_ranks):
    width = calibration.shape[1]
    rmax = sketch.shape[1]
    turned_x = turn(calibration)
    parts = gather_plane(turned_x[: width // 2], 0) + gather_plane(turned_x[width // 2 :], 1)
    sketch_t = sketch.reshape(width // NB, NB, rmax).transpose(0, 2, 1)
    tile_block = lax.all_to_all(weights, "tile", split_axis=1, concat_axis=0, tiled=True)
    sketched_t = whiten(parts, sketch_t)
    turned, basis = basis_of(tile_ranks, tile_block, sketched_t)
    served = lax.all_to_all(basis, "tile", split_axis=0, concat_axis=1, tiled=True)
    coeffs = jnp.dot(turned.reshape(rmax, width), tile_block, preferred_element_type=F32) / math.sqrt(width)
    return (served, coeffs.astype(BF16))


def solution(mesh):
    placed = (P("dp", "tile"), P("tile", None), P(("dp", "tile"), None), P("dp", "tile"))
    return jax.shard_map(
        local,
        mesh=mesh,
        in_specs=placed,
        out_specs=(P(("dp", "tile"), None), P("dp", "tile")),
        check_vma=False,
    )
```

```python
import functools
import math

import jax
import jax.numpy as jnp
from jax import lax
from jax.experimental import pallas as pl
from jax.experimental.pallas import tpu as pltpu
from jax.sharding import PartitionSpec as P

DAMPING = 0.1
NB = 128
STRIP = 8
F32 = jnp.float32
BF16 = jnp.bfloat16

NT = (((1,), (1,)), ((), ()))
NN = (((1,), (0,)), ((), ()))


def dot(a, b, dims):
    return lax.dot_general(a, b, dims, preferred_element_type=F32)


def split2(x):
    hi = x.astype(BF16)
    lo = (x - hi.astype(F32)).astype(BF16)
    return hi, lo


def split3(x):
    hi = x.astype(BF16)
    rest = x - hi.astype(F32)
    mid = rest.astype(BF16)
    lo = (rest - mid.astype(F32)).astype(BF16)
    return hi, mid, lo


def dot3(a, b, dims):
    ah, al = split2(a)
    bh, bl = split2(b)
    return dot(ah, bh, dims) + (dot(ah, bl, dims) + dot(al, bh, dims))


def dot6(a, b, dims):
    ah, am, al = split3(a)
    bh, bm, bl = split3(b)
    small = dot(am, bm, dims) + (dot(ah, bl, dims) + dot(al, bh, dims))
    return dot(ah, bh, dims) + ((dot(ah, bm, dims) + dot(am, bh, dims)) + small)


def inverse_factor(rows):
    shape = rows[0].shape
    lane = lax.broadcasted_iota(jnp.int32, shape, 1)
    sub = lax.broadcasted_iota(jnp.int32, shape, 0)
    rows = list(rows)
    out = []

    def columns(strip, base):
        return [jnp.broadcast_to(strip[:, base + k : base + k + 1], shape) for k in range(STRIP)]

    for s in range(len(rows)):
        base = s * STRIP
        strip = rows[s]
        last = s + 1 == len(rows)
        cols = columns(strip, base)
        a = [
            [jnp.broadcast_to(cols[k][i : i + 1, :], shape) if i >= k else None for k in range(STRIP)]
            for i in range(STRIP)
        ]
        own = (lane >= base) & (lane < base + STRIP)
        held = jnp.where(own, jnp.where(lane - base == sub, 1.0, 0.0), strip)
        y = [jnp.broadcast_to(held[k : k + 1, :], shape) for k in range(STRIP)]
        if not last:
            below = columns(rows[s + 1], base)
            near = jnp.where(own, 0.0, rows[s + 1])
        z = []
        low = [[None] * STRIP for _ in range(STRIP)]
        done = jnp.zeros(shape, F32)
        for k in range(STRIP):
            r = pl.reciprocal(a[k][k], approx=True)
            for i in range(k + 1, STRIP):
                low[i][k] = a[i][k] * r
                for j in range(k + 1, i + 1):
                    a[i][j] = a[i][j] - low[i][k] * a[j][k]
            for i in range(k + 1, STRIP):
                y[i] = y[i] - low[i][k] * y[k]
            if not last:
                low_near = below[k] * r
                for j in range(k + 1, STRIP):
                    below[j] = below[j] - low_near * a[j][k]
                near = near - low_near * y[k]
            z.append(y[k] * r)
            done = jnp.where(sub == k, y[k] * lax.rsqrt(a[k][k]), done)
        out.append(jnp.where(lane < base + STRIP, done, 0.0))
        if last:
            break
        rows[s + 1] = near
        for k in range(STRIP - 1, -1, -1):
            for i in range(k):
                z[i] = z[i] - low[k][i] * z[k]
        for t in range(s + 2, len(rows)):
            taken = columns(rows[t], base)
            total = jnp.where(own, 0.0, rows[t])
            for k in range(STRIP - 1, -1, -1):
                total = total - taken[k] * z[k]
            rows[t] = total
    return out


def factor_into(strips, inv_ref):
    for s, rows in enumerate(inverse_factor(strips)):
        inv_ref[s * STRIP : (s + 1) * STRIP, :] = rows


def turn_kernel(x_ref, out_ref):
    out_ref[...] = x_ref[...].T


def turn(x):
    return pl.pallas_call(
        turn_kernel,
        out_shape=jax.ShapeDtypeStruct((x.shape[1], x.shape[0]), x.dtype),
        in_specs=[pl.BlockSpec(memory_space=pltpu.VMEM)],
        out_specs=pl.BlockSpec(memory_space=pltpu.VMEM),
    )(x)


def gather_plane(half, axes):
    for axis in axes:
        side = lax.axis_size(axis)
        repeated = jnp.broadcast_to(half[None], (side,) + half.shape)
        half = lax.all_to_all(repeated, axis, split_axis=0, concat_axis=0, tiled=True)
    return half


def whiten_kernel(first, second, sketch_ref, out_ref, a_ref, d_ref, inv_ref, acc_ref):
    outer, inner, half, _ = first.shape
    width = 2 * half
    panels = width // NB
    wide = 2 * NB

    def pair(x, y, upper):
        parts = [first[y, x + d] if upper else second[x + d, y] for d in range(2)]
        return jnp.concatenate(parts, axis=1)

    for c in range(panels // 2):
        lo = c * wide
        top = bottom = None
        for x in range(0, inner, 2):
            for y in range(outer):
                low_part = pair(x, y, False)
                if lo < half:
                    high_part = pair(x, y, True)
                    right = high_part[lo : lo + wide, :]
                    term = dot(high_part[lo:, :], right, NT)
                    top = term if top is None else top + term
                    term = dot(low_part, right, NT)
                else:
                    at = lo - half
                    term = dot(low_part[at:, :], low_part[at : at + wide, :], NT)
                bottom = term if bottom is None else bottom + term
        if lo < half:
            a_ref[2 * c, lo:half, :] = top[:, :NB]
            a_ref[2 * c + 1, lo:half, :] = top[:, NB:]
        from_row = max(lo, half)
        a_ref[2 * c, from_row:, :] = bottom[:, :NB]
        a_ref[2 * c + 1, from_row:, :] = bottom[:, NB:]

    lane = lax.broadcasted_iota(jnp.int32, (NB, NB), 1)
    sub = lax.broadcasted_iota(jnp.int32, (NB, NB), 0)
    diag = lane == sub
    trace = jnp.zeros((NB, NB), F32)
    for c in range(panels):
        trace = trace + jnp.where(diag, a_ref[c, c * NB : (c + 1) * NB, :], 0.0)
    damp = jnp.sum(trace) * (DAMPING / width)
    for c in range(panels):
        block = a_ref[c, c * NB : (c + 1) * NB, :]
        a_ref[c, c * NB : (c + 1) * NB, :] = jnp.where(diag, block + damp, block)

    inv_ref[...] = jnp.zeros_like(inv_ref)
    acc_ref[...] = jnp.zeros_like(acc_ref)
    d_ref[...] = a_ref[0, :NB, :]

    tall_row = lax.broadcasted_iota(jnp.int32, (width, NB), 0)
    tall_lane = lax.broadcasted_iota(jnp.int32, (width, NB), 1)

    def panel_of(p, inv):
        ih, il = split2(inv)
        ph, pm = split2(a_ref[p])
        panel = dot(jnp.concatenate([ph, pm], axis=1), jnp.concatenate([ih, ih], axis=1), NT) + dot(ph, il, NT)
        return jnp.where(tall_row >= tall_lane + p * NB, panel, 0.0)

    def sketch_in(p, both):
        part = sketch_ref[p]
        acc_ref[...] += dot(jnp.concatenate([part, part], axis=1), both, NT)

    def step(p, carry):
        strips = [d_ref[s * STRIP : (s + 1) * STRIP, :] for s in range(NB // STRIP)]
        before = jnp.maximum(p - 1, 0)
        panel = panel_of(before, inv_ref[...])
        hi, lo16 = split2(panel)
        both = jnp.concatenate([hi, lo16], axis=1)
        right = tall_row >= p * NB
        hi_r = jnp.where(right, panel, 0.0).astype(BF16)
        lo_r = jnp.where(right, panel - hi.astype(F32), 0.0).astype(BF16)
        twice = jnp.concatenate([hi_r, hi_r], axis=1)
        for c in range(panels // 2):
            lo = c * wide
            off = dot(both[lo:], twice[lo : lo + wide], NT) + dot(hi[lo:], lo_r[lo : lo + wide], NT)
            a_ref[2 * c, lo:, :] -= off[:, :NB]
            a_ref[2 * c + 1, lo:, :] -= off[:, NB:]
        sketch_in(before, both)
        factor_into(strips, inv_ref)
        nxt = jnp.minimum(p + 1, panels - 1)
        rows_n = pl.ds(pl.multiple_of(nxt * NB, NB), NB)
        near = dot3(a_ref[p, rows_n, :], inv_ref[...], NT)
        d_ref[...] = a_ref[nxt, rows_n, :] - dot3(near, near, NT)
        return carry

    lax.fori_loop(0, panels, step, 0)
    hi, lo16 = split2(panel_of(panels - 1, inv_ref[...]))
    sketch_in(panels - 1, jnp.concatenate([hi, lo16], axis=1))
    out_ref[...] = acc_ref[...].astype(BF16)


def whiten(first, second, sketch_t):
    width = 2 * first.shape[2]
    panels, rmax, _ = sketch_t.shape
    return pl.pallas_call(
        whiten_kernel,
        out_shape=jax.ShapeDtypeStruct((rmax, width), BF16),
        in_specs=[pl.BlockSpec(memory_space=pltpu.VMEM)] * 3,
        out_specs=pl.BlockSpec(memory_space=pltpu.VMEM),
        scratch_shapes=[
            pltpu.VMEM((panels, width, NB), F32),
            pltpu.VMEM((NB, NB), F32),
            pltpu.VMEM((NB, NB), F32),
            pltpu.VMEM((rmax, width), F32),
        ],
        compiler_params=pltpu.CompilerParams(vmem_limit_bytes=40 * 1024 * 1024),
    )(first, second, sketch_t)


def basis_kernel(rank_ref, w_ref, sk_ref, turned_ref, basis_ref, t_ref, d_ref, off_ref, inv_ref):
    width = w_ref.shape[0]
    rmax = sk_ref.shape[0]
    rank = rank_ref[0, 0]
    kept = lax.broadcasted_iota(jnp.int32, sk_ref.shape, 0) < rank
    masked = jnp.where(kept, sk_ref[...].astype(F32), 0.0).astype(BF16)
    rows = dot(masked, w_ref[...], NT)
    inner = dot6(rows, rows, NT)
    sub = lax.broadcasted_iota(jnp.int32, (rmax, rmax), 0)
    lane = lax.broadcasted_iota(jnp.int32, (rmax, rmax), 1)
    inner = inner + jnp.where((sub == lane) & (sub >= rank), 1.0, 0.0)
    t_ref[0] = rows[:NB]
    t_ref[1] = rows[NB:]
    d_ref[0] = inner[:NB, :NB]
    d_ref[1] = inner[NB:, NB:]
    off_ref[...] = inner[NB:, :NB]

    def step(p, carry):
        factor_into([d_ref[p, s * STRIP : (s + 1) * STRIP, :] for s in range(NB // STRIP)], inv_ref)
        inv = inv_ref[...]
        base = dot3(inv, t_ref[p], NN)
        low = dot6(off_ref[...], inv, NT)
        d_ref[1] = d_ref[1] - dot6(low, low, NT)
        t_ref[1] = t_ref[1] - dot6(low, base, NN)
        scaled = base * math.sqrt(width)
        turned_ref[p] = scaled.astype(BF16)
        basis_ref[:, pl.ds(pl.multiple_of(p * NB, NB), NB)] = scaled.T.astype(BF16)
        return carry

    lax.fori_loop(0, rmax // NB, step, 0)


def basis_of(rank, tile_block, sketched_t):
    width = tile_block.shape[0]
    rmax = sketched_t.shape[0]
    halves = rmax // NB
    return pl.pallas_call(
        basis_kernel,
        out_shape=(
            jax.ShapeDtypeStruct((halves, NB, width), BF16),
            jax.ShapeDtypeStruct((width, rmax), BF16),
        ),
        in_specs=[
            pl.BlockSpec(memory_space=pltpu.SMEM),
            pl.BlockSpec(memory_space=pltpu.VMEM),
            pl.BlockSpec(memory_space=pltpu.VMEM),
        ],
        out_specs=(pl.BlockSpec(memory_space=pltpu.VMEM),) * 2,
        scratch_shapes=[
            pltpu.VMEM((halves, NB, width), F32),
            pltpu.VMEM((halves, NB, NB), F32),
            pltpu.VMEM((NB, NB), F32),
            pltpu.VMEM((NB, NB), F32),
        ],
        compiler_params=pltpu.CompilerParams(vmem_limit_bytes=40 * 1024 * 1024),
    )(rank, tile_block, sketched_t)


def local(calibration, sketch, weights, tile_ranks):
    width = calibration.shape[1]
    rmax = sketch.shape[1]
    turned_x = turn(calibration)
    first = gather_plane(turned_x[: width // 2], ("x", "y"))
    second = gather_plane(turned_x[width // 2 :], ("y", "x"))
    sketch_t = sketch.reshape(width // NB, NB, rmax).transpose(0, 2, 1)
    tile_block = lax.all_to_all(weights, "tile", split_axis=1, concat_axis=0, tiled=True)
    sketched_t = whiten(first, second, sketch_t)
    turned, basis = basis_of(tile_ranks, tile_block, sketched_t)
    served = lax.all_to_all(basis, "tile", split_axis=0, concat_axis=1, tiled=True)
    coeffs = jnp.dot(turned.reshape(rmax, width), tile_block, preferred_element_type=F32) / math.sqrt(width)
    return (served, coeffs.astype(BF16))


def solution(mesh):
    tokens, tiles = mesh.devices.shape
    side = math.isqrt(tokens)
    plane = jax.sharding.Mesh(mesh.devices.reshape(side, side, tiles), ("x", "y", "tile"))
    dp = ("x", "y")
    return jax.shard_map(
        local,
        mesh=plane,
        in_specs=(P(dp, "tile"), P("tile", None), P((*dp, "tile"), None), P(dp, "tile")),
        out_specs=(P((*dp, "tile"), None), P(dp, "tile")),
        check_vma=False,
    )
```

```python
import functools
import math

import jax
import jax.numpy as jnp
from jax import lax
from jax.experimental import pallas as pl
from jax.experimental.pallas import tpu as pltpu
from jax.sharding import PartitionSpec as P

DAMPING = 0.1
NB = 128
STRIP = 8
F32 = jnp.float32
BF16 = jnp.bfloat16

NT = (((1,), (1,)), ((), ()))
NN = (((1,), (0,)), ((), ()))


def dot(a, b, dims):
    return lax.dot_general(a, b, dims, preferred_element_type=F32)


def split2(x):
    hi = x.astype(BF16)
    lo = (x - hi.astype(F32)).astype(BF16)
    return hi, lo


def split3(x):
    hi = x.astype(BF16)
    rest = x - hi.astype(F32)
    mid = rest.astype(BF16)
    lo = (rest - mid.astype(F32)).astype(BF16)
    return hi, mid, lo


def dot3(a, b, dims):
    ah, al = split2(a)
    bh, bl = split2(b)
    return dot(ah, bh, dims) + (dot(ah, bl, dims) + dot(al, bh, dims))


def dot6(a, b, dims):
    ah, am, al = split3(a)
    bh, bm, bl = split3(b)
    small = dot(am, bm, dims) + (dot(ah, bl, dims) + dot(al, bh, dims))
    return dot(ah, bh, dims) + ((dot(ah, bm, dims) + dot(am, bh, dims)) + small)


def inverse_factor(rows):
    shape = rows[0].shape
    lane = lax.broadcasted_iota(jnp.int32, shape, 1)
    sub = lax.broadcasted_iota(jnp.int32, shape, 0)
    rows = list(rows)
    out = []

    def columns(strip, base):
        return [jnp.broadcast_to(strip[:, base + k : base + k + 1], shape) for k in range(STRIP)]

    for s in range(len(rows)):
        base = s * STRIP
        strip = rows[s]
        last = s + 1 == len(rows)
        cols = columns(strip, base)
        a = [
            [jnp.broadcast_to(cols[k][i : i + 1, :], shape) if i >= k else None for k in range(STRIP)]
            for i in range(STRIP)
        ]
        own = (lane >= base) & (lane < base + STRIP)
        held = jnp.where(own, jnp.where(lane - base == sub, 1.0, 0.0), strip)
        y = [jnp.broadcast_to(held[k : k + 1, :], shape) for k in range(STRIP)]
        if not last:
            below = columns(rows[s + 1], base)
            near = jnp.where(own, 0.0, rows[s + 1])
        z = []
        low = [[None] * STRIP for _ in range(STRIP)]
        done = jnp.zeros(shape, F32)
        for k in range(STRIP):
            r = pl.reciprocal(a[k][k], approx=True)
            for i in range(k + 1, STRIP):
                low[i][k] = a[i][k] * r
                for j in range(k + 1, i + 1):
                    a[i][j] = a[i][j] - low[i][k] * a[j][k]
            for i in range(k + 1, STRIP):
                y[i] = y[i] - low[i][k] * y[k]
            if not last:
                low_near = below[k] * r
                for j in range(k + 1, STRIP):
                    below[j] = below[j] - low_near * a[j][k]
                near = near - low_near * y[k]
            z.append(y[k] * r)
            done = jnp.where(sub == k, y[k] * lax.rsqrt(a[k][k]), done)
        out.append(jnp.where(lane < base + STRIP, done, 0.0))
        if last:
            break
        rows[s + 1] = near
        for k in range(STRIP - 1, -1, -1):
            for i in range(k):
                z[i] = z[i] - low[k][i] * z[k]
        for t in range(s + 2, len(rows)):
            taken = columns(rows[t], base)
            total = jnp.where(own, 0.0, rows[t])
            for k in range(STRIP - 1, -1, -1):
                total = total - taken[k] * z[k]
            rows[t] = total
    return out


def factor_into(strips, inv_ref):
    for s, rows in enumerate(inverse_factor(strips)):
        inv_ref[s * STRIP : (s + 1) * STRIP, :] = rows


def prepare_kernel(x_ref, w_ref, high_ref, low_ref, pieces_ref, sems):
    pieces, _, width = pieces_ref.shape
    copies = [
        pltpu.make_async_copy(w_ref.at[:, pl.ds(t * width, width)], pieces_ref.at[t], sems.at[t]) for t in range(pieces)
    ]
    for copy in copies:
        copy.start()
    half = high_ref.shape[0]
    high_ref[...] = x_ref[:, :half].T
    low_ref[...] = x_ref[:, half:].T
    for copy in copies:
        copy.wait()


def prepare(x, weights):
    tokens, width = x.shape
    rows, columns = weights.shape
    pieces = columns // width
    half = jax.ShapeDtypeStruct((width // 2, tokens), x.dtype)
    return pl.pallas_call(
        prepare_kernel,
        out_shape=(half, half, jax.ShapeDtypeStruct((pieces, rows, width), weights.dtype)),
        in_specs=[pl.BlockSpec(memory_space=pltpu.VMEM), pl.BlockSpec(memory_space=pltpu.HBM)],
        out_specs=(
            pl.BlockSpec(memory_space=pltpu.VMEM),
            pl.BlockSpec(memory_space=pltpu.VMEM),
            pl.BlockSpec(memory_space=pl.ANY),
        ),
        scratch_shapes=[pltpu.SemaphoreType.DMA((pieces,))],
    )(x, weights)


def shifted(value, axis, shift):
    side = lax.axis_size(axis)
    return lax.ppermute(value, axis, [(i, (i + shift) % side) for i in range(side)])


def gather_plane(half, axes):
    line = jnp.stack([half] + [shifted(half, axes[0], d) for d in (2, 1, -1)])
    return (line,) + tuple(shifted(line, axes[1], d) for d in (2, 1, -1))


def whiten_kernel(*refs):
    first, second = refs[:4], refs[4:8]
    sketch_ref, out_ref, a_ref, d_ref, inv_ref, acc_ref = refs[8:]
    outer = len(first)
    inner, half, _ = first[0].shape
    width = 2 * half
    panels = width // NB
    wide = 2 * NB

    def pair(x, y, upper):
        parts = [first[y][x + d] if upper else second[x + d][y] for d in range(2)]
        return jnp.concatenate(parts, axis=1)

    for c in range(panels // 2):
        lo = c * wide
        top = bottom = None
        for x in range(0, inner, 2):
            for y in range(outer):
                low_part = pair(x, y, False)
                if lo < half:
                    high_part = pair(x, y, True)
                    right = high_part[lo : lo + wide, :]
                    term = dot(high_part[lo:, :], right, NT)
                    top = term if top is None else top + term
                    term = dot(low_part, right, NT)
                else:
                    at = lo - half
                    term = dot(low_part[at:, :], low_part[at : at + wide, :], NT)
                bottom = term if bottom is None else bottom + term
        if lo < half:
            a_ref[2 * c, lo:half, :] = top[:, :NB]
            a_ref[2 * c + 1, lo:half, :] = top[:, NB:]
        from_row = max(lo, half)
        a_ref[2 * c, from_row:, :] = bottom[:, :NB]
        a_ref[2 * c + 1, from_row:, :] = bottom[:, NB:]

    lane = lax.broadcasted_iota(jnp.int32, (NB, NB), 1)
    sub = lax.broadcasted_iota(jnp.int32, (NB, NB), 0)
    diag = lane == sub
    trace = jnp.zeros((NB, NB), F32)
    for c in range(panels):
        trace = trace + jnp.where(diag, a_ref[c, c * NB : (c + 1) * NB, :], 0.0)
    damp = jnp.sum(trace) * (DAMPING / width)
    for c in range(panels):
        block = a_ref[c, c * NB : (c + 1) * NB, :]
        a_ref[c, c * NB : (c + 1) * NB, :] = jnp.where(diag, block + damp, block)

    inv_ref[...] = jnp.zeros_like(inv_ref)
    acc_ref[...] = jnp.zeros_like(acc_ref)
    d_ref[...] = a_ref[0, :NB, :]

    tall_row = lax.broadcasted_iota(jnp.int32, (width, NB), 0)
    tall_lane = lax.broadcasted_iota(jnp.int32, (width, NB), 1)

    def panel_of(p, inv):
        ih, il = split2(inv)
        ph, pm = split2(a_ref[p])
        panel = dot(jnp.concatenate([ph, pm], axis=1), jnp.concatenate([ih, ih], axis=1), NT) + dot(ph, il, NT)
        return jnp.where(tall_row >= tall_lane + p * NB, panel, 0.0)

    def sketch_in(p, both):
        part = sketch_ref[p]
        acc_ref[...] += dot(jnp.concatenate([part, part], axis=1), both, NT)

    def step(p, carry):
        strips = [d_ref[s * STRIP : (s + 1) * STRIP, :] for s in range(NB // STRIP)]
        before = jnp.maximum(p - 1, 0)
        panel = panel_of(before, inv_ref[...])
        hi, lo16 = split2(panel)
        both = jnp.concatenate([hi, lo16], axis=1)
        right = tall_row >= p * NB
        hi_r = jnp.where(right, panel, 0.0).astype(BF16)
        lo_r = jnp.where(right, panel - hi.astype(F32), 0.0).astype(BF16)
        twice = jnp.concatenate([hi_r, hi_r], axis=1)
        for c in range(panels // 2):
            lo = c * wide
            off = dot(both[lo:], twice[lo : lo + wide], NT) + dot(hi[lo:], lo_r[lo : lo + wide], NT)
            a_ref[2 * c, lo:, :] -= off[:, :NB]
            a_ref[2 * c + 1, lo:, :] -= off[:, NB:]
        sketch_in(before, both)
        factor_into(strips, inv_ref)
        nxt = jnp.minimum(p + 1, panels - 1)
        rows_n = pl.ds(pl.multiple_of(nxt * NB, NB), NB)
        near = dot3(a_ref[p, rows_n, :], inv_ref[...], NT)
        d_ref[...] = a_ref[nxt, rows_n, :] - dot3(near, near, NT)
        return carry

    lax.fori_loop(0, panels, step, 0)
    hi, lo16 = split2(panel_of(panels - 1, inv_ref[...]))
    sketch_in(panels - 1, jnp.concatenate([hi, lo16], axis=1))
    out_ref[...] = acc_ref[...].astype(BF16)


def whiten(first, second, sketch_t):
    width = 2 * first[0].shape[1]
    panels, rmax, _ = sketch_t.shape
    return pl.pallas_call(
        whiten_kernel,
        out_shape=jax.ShapeDtypeStruct((rmax, width), BF16),
        in_specs=[pl.BlockSpec(memory_space=pltpu.VMEM)] * 9,
        out_specs=pl.BlockSpec(memory_space=pltpu.VMEM),
        scratch_shapes=[
            pltpu.VMEM((panels, width, NB), F32),
            pltpu.VMEM((NB, NB), F32),
            pltpu.VMEM((NB, NB), F32),
            pltpu.VMEM((rmax, width), F32),
        ],
        compiler_params=pltpu.CompilerParams(vmem_limit_bytes=24 * 1024 * 1024),
    )(*first, *second, sketch_t)


def basis_kernel(rank_ref, w_ref, sk_ref, turned_ref, basis_ref, first_inv, second_inv):
    width = w_ref.shape[0]
    rmax = sk_ref.shape[0]
    rank = rank_ref[0, 0]
    kept = lax.broadcasted_iota(jnp.int32, sk_ref.shape, 0) < rank
    masked = jnp.where(kept, sk_ref[...].astype(F32), 0.0).astype(BF16)
    rows = dot(masked, w_ref[...], NT)
    inner = dot6(rows, rows, NT)
    sub = lax.broadcasted_iota(jnp.int32, (rmax, rmax), 0)
    lane = lax.broadcasted_iota(jnp.int32, (rmax, rmax), 1)
    inner = inner + jnp.where((sub == lane) & (sub >= rank), 1.0, 0.0)
    inv_ref = (first_inv, second_inv)

    def factor(block, p):
        factor_into([block[s * STRIP : (s + 1) * STRIP] for s in range(NB // STRIP)], inv_ref[p])
        return inv_ref[p][...]

    def put(base, p):
        scaled = base * math.sqrt(width)
        turned_ref[p * NB : (p + 1) * NB, :] = scaled.astype(BF16)
        basis_ref[:, p * NB : (p + 1) * NB] = scaled.T.astype(BF16)

    inv = factor(inner[:NB, :NB], 0)
    low = dot6(inner[NB:, :NB], inv, NT)
    rest = inner[NB:, NB:] - dot6(low, low, NT)
    base = dot3(inv, rows[:NB], NN)
    left = rows[NB:] - dot3(low, base, NN)
    put(base, 0)
    put(dot3(factor(rest, 1), left, NN), 1)


def basis_of(rank, tile_block, sketched_t):
    width = tile_block.shape[0]
    rmax = sketched_t.shape[0]
    return pl.pallas_call(
        basis_kernel,
        out_shape=(
            jax.ShapeDtypeStruct((rmax, width), BF16),
            jax.ShapeDtypeStruct((width, rmax), BF16),
        ),
        in_specs=[
            pl.BlockSpec(memory_space=pltpu.SMEM),
            pl.BlockSpec(memory_space=pltpu.VMEM),
            pl.BlockSpec(memory_space=pltpu.VMEM),
        ],
        out_specs=(pl.BlockSpec(memory_space=pltpu.VMEM),) * 2,
        scratch_shapes=[
            pltpu.VMEM((NB, NB), F32),
            pltpu.VMEM((NB, NB), F32),
        ],
        compiler_params=pltpu.CompilerParams(vmem_limit_bytes=24 * 1024 * 1024),
    )(rank, tile_block, sketched_t)


def local(calibration, sketch, weights, tile_ranks):
    width = calibration.shape[1]
    rmax = sketch.shape[1]
    high, low, pieces = prepare(calibration, weights)
    tile_block = lax.all_to_all(pieces, "tile", split_axis=0, concat_axis=0, tiled=True).reshape(width, width)
    first = gather_plane(high, ("x", "y"))
    second = gather_plane(low, ("y", "x"))
    sketch_t = sketch.reshape(width // NB, NB, rmax).transpose(0, 2, 1)
    sketched_t = whiten(first, second, sketch_t)
    turned, basis = basis_of(tile_ranks, tile_block, sketched_t)
    served = lax.all_to_all(basis, "tile", split_axis=0, concat_axis=1, tiled=True)
    coeffs = jnp.dot(turned, tile_block, preferred_element_type=F32) / math.sqrt(width)
    return (served, coeffs.astype(BF16))


def solution(mesh):
    tokens, tiles = mesh.devices.shape
    side = math.isqrt(tokens)
    plane = jax.sharding.Mesh(mesh.devices.reshape(side, side, tiles), ("x", "y", "tile"))
    dp = ("x", "y")
    return jax.shard_map(
        local,
        mesh=plane,
        in_specs=(P(dp, "tile"), P("tile", None), P((*dp, "tile"), None), P(dp, "tile")),
        out_specs=(P((*dp, "tile"), None), P(dp, "tile")),
        check_vma=False,
    )
```

```python
import functools
import math

import jax
import jax.numpy as jnp
from jax import lax
from jax.experimental import pallas as pl
from jax.experimental.pallas import tpu as pltpu
from jax.sharding import PartitionSpec as P

DAMPING = 0.1
NB = 128
STRIP = 8
F32 = jnp.float32
BF16 = jnp.bfloat16

NT = (((1,), (1,)), ((), ()))
NN = (((1,), (0,)), ((), ()))


def dot(a, b, dims):
    return lax.dot_general(a, b, dims, preferred_element_type=F32)


def split2(x):
    hi = x.astype(BF16)
    lo = (x - hi.astype(F32)).astype(BF16)
    return hi, lo


def split3(x):
    hi = x.astype(BF16)
    rest = x - hi.astype(F32)
    mid = rest.astype(BF16)
    lo = (rest - mid.astype(F32)).astype(BF16)
    return hi, mid, lo


def dot3(a, b, dims):
    ah, al = split2(a)
    bh, bl = split2(b)
    return dot(ah, bh, dims) + (dot(ah, bl, dims) + dot(al, bh, dims))


def dot6(a, b, dims):
    ah, am, al = split3(a)
    bh, bm, bl = split3(b)
    small = dot(am, bm, dims) + (dot(ah, bl, dims) + dot(al, bh, dims))
    return dot(ah, bh, dims) + ((dot(ah, bm, dims) + dot(am, bh, dims)) + small)


def inverse_factor(rows):
    shape = rows[0].shape
    lane = lax.broadcasted_iota(jnp.int32, shape, 1)
    sub = lax.broadcasted_iota(jnp.int32, shape, 0)
    rows = list(rows)
    out = []

    def columns(strip, base):
        return [jnp.broadcast_to(strip[:, base + k : base + k + 1], shape) for k in range(STRIP)]

    for s in range(len(rows)):
        base = s * STRIP
        strip = rows[s]
        last = s + 1 == len(rows)
        cols = columns(strip, base)
        a = [
            [jnp.broadcast_to(cols[k][i : i + 1, :], shape) if i >= k else None for k in range(STRIP)]
            for i in range(STRIP)
        ]
        own = (lane >= base) & (lane < base + STRIP)
        held = jnp.where(own, jnp.where(lane - base == sub, 1.0, 0.0), strip)
        y = [jnp.broadcast_to(held[k : k + 1, :], shape) for k in range(STRIP)]
        if not last:
            below = columns(rows[s + 1], base)
            near = jnp.where(own, 0.0, rows[s + 1])
        z = []
        low = [[None] * STRIP for _ in range(STRIP)]
        done = jnp.zeros(shape, F32)
        for k in range(STRIP):
            r = pl.reciprocal(a[k][k], approx=True)
            for i in range(k + 1, STRIP):
                low[i][k] = a[i][k] * r
                for j in range(k + 1, i + 1):
                    a[i][j] = a[i][j] - low[i][k] * a[j][k]
            for i in range(k + 1, STRIP):
                y[i] = y[i] - low[i][k] * y[k]
            if not last:
                low_near = below[k] * r
                for j in range(k + 1, STRIP):
                    below[j] = below[j] - low_near * a[j][k]
                near = near - low_near * y[k]
            z.append(y[k] * r)
            done = jnp.where(sub == k, y[k] * lax.rsqrt(a[k][k]), done)
        out.append(jnp.where(lane < base + STRIP, done, 0.0))
        if last:
            break
        rows[s + 1] = near
        for k in range(STRIP - 1, -1, -1):
            for i in range(k):
                z[i] = z[i] - low[k][i] * z[k]
        for t in range(s + 2, len(rows)):
            taken = columns(rows[t], base)
            total = jnp.where(own, 0.0, rows[t])
            for k in range(STRIP - 1, -1, -1):
                total = total - taken[k] * z[k]
            rows[t] = total
    return out


def factor_into(strips, inv_ref):
    for s, rows in enumerate(inverse_factor(strips)):
        inv_ref[s * STRIP : (s + 1) * STRIP, :] = rows


def prepare_kernel(x_ref, w_ref, high_ref, low_ref, pieces_ref, sems):
    pieces, _, width = pieces_ref.shape
    copies = [
        pltpu.make_async_copy(w_ref.at[:, pl.ds(t * width, width)], pieces_ref.at[t], sems.at[t]) for t in range(pieces)
    ]
    for copy in copies:
        copy.start()
    half = high_ref.shape[0]
    high_ref[...] = x_ref[:, :half].T
    low_ref[...] = x_ref[:, half:].T
    for copy in copies:
        copy.wait()


def prepare(x, weights):
    tokens, width = x.shape
    rows, columns = weights.shape
    pieces = columns // width
    half = jax.ShapeDtypeStruct((width // 2, tokens), x.dtype)
    return pl.pallas_call(
        prepare_kernel,
        out_shape=(half, half, jax.ShapeDtypeStruct((pieces, rows, width), weights.dtype)),
        in_specs=[pl.BlockSpec(memory_space=pltpu.VMEM), pl.BlockSpec(memory_space=pltpu.HBM)],
        out_specs=(pl.BlockSpec(memory_space=pltpu.VMEM),) * 3,
        scratch_shapes=[pltpu.SemaphoreType.DMA((pieces,))],
        compiler_params=pltpu.CompilerParams(vmem_limit_bytes=16 * 1024 * 1024),
    )(x, weights)


def shifted(value, axis, shift):
    side = lax.axis_size(axis)
    return lax.ppermute(value, axis, [(i, (i + shift) % side) for i in range(side)])


FAR_FIRST = (2, 1, -1)


def gather_plane(high, low):
    lines = [tuple(shifted(half, axis, d) for d in FAR_FIRST) for half, axis in ((high, "x"), (low, "y"))]
    lines = lax.optimization_barrier(lines)
    lines = [jnp.stack((half,) + line) for half, line in zip((high, low), lines)]
    return [(line,) + tuple(shifted(line, axis, d) for d in FAR_FIRST) for line, axis in zip(lines, ("y", "x"))]


def whiten_kernel(*refs):
    first, second = refs[:4], refs[4:8]
    sketch_ref, out_ref, a_ref, d_ref, inv_ref, acc_ref = refs[8:]
    outer = len(first)
    inner, half, _ = first[0].shape
    width = 2 * half
    panels = width // NB
    wide = 2 * NB

    def pair(x, y, upper):
        parts = [first[y][x + d] if upper else second[x + d][y] for d in range(2)]
        return jnp.concatenate(parts, axis=1)

    for c in range(panels // 2):
        lo = c * wide
        top = bottom = None
        for x in range(0, inner, 2):
            for y in range(outer):
                low_part = pair(x, y, False)
                if lo < half:
                    high_part = pair(x, y, True)
                    right = high_part[lo : lo + wide, :]
                    term = dot(high_part[lo:, :], right, NT)
                    top = term if top is None else top + term
                    term = dot(low_part, right, NT)
                else:
                    at = lo - half
                    term = dot(low_part[at:, :], low_part[at : at + wide, :], NT)
                bottom = term if bottom is None else bottom + term
        if lo < half:
            a_ref[2 * c, lo:half, :] = top[:, :NB]
            a_ref[2 * c + 1, lo:half, :] = top[:, NB:]
        from_row = max(lo, half)
        a_ref[2 * c, from_row:, :] = bottom[:, :NB]
        a_ref[2 * c + 1, from_row:, :] = bottom[:, NB:]

    lane = lax.broadcasted_iota(jnp.int32, (NB, NB), 1)
    sub = lax.broadcasted_iota(jnp.int32, (NB, NB), 0)
    diag = lane == sub
    trace = jnp.zeros((NB, NB), F32)
    for c in range(panels):
        trace = trace + jnp.where(diag, a_ref[c, c * NB : (c + 1) * NB, :], 0.0)
    damp = jnp.sum(trace) * (DAMPING / width)
    for c in range(panels):
        block = a_ref[c, c * NB : (c + 1) * NB, :]
        a_ref[c, c * NB : (c + 1) * NB, :] = jnp.where(diag, block + damp, block)

    inv_ref[...] = jnp.zeros_like(inv_ref)
    acc_ref[...] = jnp.zeros_like(acc_ref)
    d_ref[...] = a_ref[0, :NB, :]

    tall_row = lax.broadcasted_iota(jnp.int32, (width, NB), 0)
    tall_lane = lax.broadcasted_iota(jnp.int32, (width, NB), 1)

    def panel_of(p, inv):
        ih, il = split2(inv)
        ph, pm = split2(a_ref[p])
        panel = dot(jnp.concatenate([ph, pm], axis=1), jnp.concatenate([ih, ih], axis=1), NT) + dot(ph, il, NT)
        return jnp.where(tall_row >= tall_lane + p * NB, panel, 0.0)

    def sketch_in(p, both):
        part = sketch_ref[p]
        acc_ref[...] += dot(jnp.concatenate([part, part], axis=1), both, NT)

    def step(p, carry):
        strips = [d_ref[s * STRIP : (s + 1) * STRIP, :] for s in range(NB // STRIP)]
        before = jnp.maximum(p - 1, 0)
        panel = panel_of(before, inv_ref[...])
        hi, lo16 = split2(panel)
        both = jnp.concatenate([hi, lo16], axis=1)
        right = tall_row >= p * NB
        hi_r = jnp.where(right, panel, 0.0).astype(BF16)
        lo_r = jnp.where(right, panel - hi.astype(F32), 0.0).astype(BF16)
        twice = jnp.concatenate([hi_r, hi_r], axis=1)
        for c in range(panels // 2):
            lo = c * wide
            off = dot(both[lo:], twice[lo : lo + wide], NT) + dot(hi[lo:], lo_r[lo : lo + wide], NT)
            a_ref[2 * c, lo:, :] -= off[:, :NB]
            a_ref[2 * c + 1, lo:, :] -= off[:, NB:]
        sketch_in(before, both)
        factor_into(strips, inv_ref)
        nxt = jnp.minimum(p + 1, panels - 1)
        rows_n = pl.ds(pl.multiple_of(nxt * NB, NB), NB)
        near = dot3(a_ref[p, rows_n, :], inv_ref[...], NT)
        d_ref[...] = a_ref[nxt, rows_n, :] - dot3(near, near, NT)
        return carry

    lax.fori_loop(0, panels, step, 0)
    hi, lo16 = split2(panel_of(panels - 1, inv_ref[...]))
    sketch_in(panels - 1, jnp.concatenate([hi, lo16], axis=1))
    out_ref[...] = acc_ref[...].astype(BF16)


def whiten(first, second, sketch_t):
    width = 2 * first[0].shape[1]
    panels, rmax, _ = sketch_t.shape
    return pl.pallas_call(
        whiten_kernel,
        out_shape=jax.ShapeDtypeStruct((rmax, width), BF16),
        in_specs=[pl.BlockSpec(memory_space=pltpu.VMEM)] * 9,
        out_specs=pl.BlockSpec(memory_space=pltpu.VMEM),
        scratch_shapes=[
            pltpu.VMEM((panels, width, NB), F32),
            pltpu.VMEM((NB, NB), F32),
            pltpu.VMEM((NB, NB), F32),
            pltpu.VMEM((rmax, width), F32),
        ],
        compiler_params=pltpu.CompilerParams(vmem_limit_bytes=24 * 1024 * 1024),
    )(*first, *second, sketch_t)


def basis_kernel(rank_ref, w_ref, sk_ref, turned_ref, basis_ref, first_inv, second_inv):
    width = w_ref.shape[0]
    rmax = sk_ref.shape[0]
    rank = rank_ref[0, 0]
    kept = lax.broadcasted_iota(jnp.int32, sk_ref.shape, 0) < rank
    masked = jnp.where(kept, sk_ref[...].astype(F32), 0.0).astype(BF16)
    rows = dot(masked, w_ref[...], NT)
    inner = dot6(rows, rows, NT)
    sub = lax.broadcasted_iota(jnp.int32, (rmax, rmax), 0)
    lane = lax.broadcasted_iota(jnp.int32, (rmax, rmax), 1)
    inner = inner + jnp.where((sub == lane) & (sub >= rank), 1.0, 0.0)
    inv_ref = (first_inv, second_inv)

    def factor(block, p):
        factor_into([block[s * STRIP : (s + 1) * STRIP] for s in range(NB // STRIP)], inv_ref[p])
        return inv_ref[p][...]

    def put(base, p):
        scaled = base * math.sqrt(width)
        turned_ref[p * NB : (p + 1) * NB, :] = scaled.astype(BF16)
        basis_ref[:, p * NB : (p + 1) * NB] = scaled.T.astype(BF16)

    inv = factor(inner[:NB, :NB], 0)
    low = dot6(inner[NB:, :NB], inv, NT)
    rest = inner[NB:, NB:] - dot6(low, low, NT)
    base = dot3(inv, rows[:NB], NN)
    left = rows[NB:] - dot3(low, base, NN)
    put(base, 0)
    put(dot3(factor(rest, 1), left, NN), 1)


def basis_of(rank, tile_block, sketched_t):
    width = tile_block.shape[0]
    rmax = sketched_t.shape[0]
    return pl.pallas_call(
        basis_kernel,
        out_shape=(
            jax.ShapeDtypeStruct((rmax, width), BF16),
            jax.ShapeDtypeStruct((width, rmax), BF16),
        ),
        in_specs=[
            pl.BlockSpec(memory_space=pltpu.SMEM),
            pl.BlockSpec(memory_space=pltpu.VMEM),
            pl.BlockSpec(memory_space=pltpu.VMEM),
        ],
        out_specs=(pl.BlockSpec(memory_space=pltpu.VMEM),) * 2,
        scratch_shapes=[
            pltpu.VMEM((NB, NB), F32),
            pltpu.VMEM((NB, NB), F32),
        ],
        compiler_params=pltpu.CompilerParams(vmem_limit_bytes=24 * 1024 * 1024),
    )(rank, tile_block, sketched_t)


def local(calibration, sketch, weights, tile_ranks):
    width = calibration.shape[1]
    rmax = sketch.shape[1]
    high, low, pieces = prepare(calibration, weights)
    tile_block = lax.all_to_all(pieces, "tile", split_axis=0, concat_axis=0, tiled=True).reshape(width, width)
    first, second = gather_plane(high, low)
    sketch_t = sketch.reshape(width // NB, NB, rmax).transpose(0, 2, 1)
    sketched_t = whiten(first, second, sketch_t)
    turned, basis = basis_of(tile_ranks, tile_block, sketched_t)
    served = lax.all_to_all(basis, "tile", split_axis=0, concat_axis=1, tiled=True)
    coeffs = jnp.dot(turned, tile_block, preferred_element_type=F32) / math.sqrt(width)
    return (served, coeffs.astype(BF16))


def solution(mesh):
    tokens, tiles = mesh.devices.shape
    side = math.isqrt(tokens)
    plane = jax.sharding.Mesh(mesh.devices.reshape(side, side, tiles), ("x", "y", "tile"))
    dp = ("x", "y")
    return jax.shard_map(
        local,
        mesh=plane,
        in_specs=(P(dp, "tile"), P("tile", None), P((*dp, "tile"), None), P(dp, "tile")),
        out_specs=(P((*dp, "tile"), None), P(dp, "tile")),
        check_vma=False,
    )
```

```python
import functools
import math

import jax
import jax.numpy as jnp
from jax import lax
from jax.experimental import pallas as pl
from jax.experimental.pallas import tpu as pltpu
from jax.sharding import PartitionSpec as P

DAMPING = 0.1
NB = 128
STRIP = 8
PREPARE_STEPS = 4
GRANT = 56 * 1024 * 1024
F32 = jnp.float32
BF16 = jnp.bfloat16

NT = (((1,), (1,)), ((), ()))
NN = (((1,), (0,)), ((), ()))


def dot(a, b, dims):
    return lax.dot_general(a, b, dims, preferred_element_type=F32)


def split2(x):
    hi = x.astype(BF16)
    lo = (x - hi.astype(F32)).astype(BF16)
    return hi, lo


def split3(x):
    hi = x.astype(BF16)
    rest = x - hi.astype(F32)
    mid = rest.astype(BF16)
    lo = (rest - mid.astype(F32)).astype(BF16)
    return hi, mid, lo


def dot3(a, b, dims):
    ah, al = split2(a)
    bh, bl = split2(b)
    return dot(ah, bh, dims) + (dot(ah, bl, dims) + dot(al, bh, dims))


def dot6(a, b, dims):
    ah, am, al = split3(a)
    bh, bm, bl = split3(b)
    small = dot(am, bm, dims) + (dot(ah, bl, dims) + dot(al, bh, dims))
    return dot(ah, bh, dims) + ((dot(ah, bm, dims) + dot(am, bh, dims)) + small)


def inverse_factor(rows):
    shape = rows[0].shape
    lane = lax.broadcasted_iota(jnp.int32, shape, 1)
    sub = lax.broadcasted_iota(jnp.int32, shape, 0)
    rows = list(rows)
    out = []

    def columns(strip, base):
        return [jnp.broadcast_to(strip[:, base + k : base + k + 1], shape) for k in range(STRIP)]

    for s in range(len(rows)):
        base = s * STRIP
        strip = rows[s]
        last = s + 1 == len(rows)
        cols = columns(strip, base)
        a = [
            [jnp.broadcast_to(cols[k][i : i + 1, :], shape) if i >= k else None for k in range(STRIP)]
            for i in range(STRIP)
        ]
        own = (lane >= base) & (lane < base + STRIP)
        held = jnp.where(own, jnp.where(lane - base == sub, 1.0, 0.0), strip)
        y = [jnp.broadcast_to(held[k : k + 1, :], shape) for k in range(STRIP)]
        if not last:
            below = columns(rows[s + 1], base)
            near = jnp.where(own, 0.0, rows[s + 1])
        z = []
        low = [[None] * STRIP for _ in range(STRIP)]
        done = jnp.zeros(shape, F32)
        for k in range(STRIP):
            r = pl.reciprocal(a[k][k], approx=True)
            for i in range(k + 1, STRIP):
                low[i][k] = a[i][k] * r
                for j in range(k + 1, i + 1):
                    a[i][j] = a[i][j] - low[i][k] * a[j][k]
            for i in range(k + 1, STRIP):
                y[i] = y[i] - low[i][k] * y[k]
            if not last:
                low_near = below[k] * r
                for j in range(k + 1, STRIP):
                    below[j] = below[j] - low_near * a[j][k]
                near = near - low_near * y[k]
            z.append(y[k] * r)
            done = jnp.where(sub == k, y[k] * lax.rsqrt(a[k][k]), done)
        out.append(jnp.where(lane < base + STRIP, done, 0.0))
        if last:
            break
        rows[s + 1] = near
        for k in range(STRIP - 1, -1, -1):
            for i in range(k):
                z[i] = z[i] - low[k][i] * z[k]
        for t in range(s + 2, len(rows)):
            taken = columns(rows[t], base)
            total = jnp.where(own, 0.0, rows[t])
            for k in range(STRIP - 1, -1, -1):
                total = total - taken[k] * z[k]
            rows[t] = total
    return out


def factor_into(strips, inv_ref):
    for s, rows in enumerate(inverse_factor(strips)):
        inv_ref[s * STRIP : (s + 1) * STRIP, :] = rows


def prepare_kernel(x_ref, w_ref, high_ref, low_ref, pieces_ref, hold_ref, in_sems, out_sems):
    pieces, _, width = hold_ref.shape
    group = pieces // PREPARE_STEPS
    inward = [
        pltpu.make_async_copy(w_ref.at[:, pl.ds(t * width, width)], hold_ref.at[t], in_sems.at[t]) for t in range(pieces)
    ]
    outward = [
        pltpu.make_async_copy(hold_ref.at[pl.ds(g * group, group)], pieces_ref.at[pl.ds(g * group, group)], out_sems.at[g])
        for g in range(PREPARE_STEPS)
    ]
    for copy in inward:
        copy.start()
    half = high_ref.shape[0]
    high_ref[...] = x_ref[:, :half].T
    low_ref[...] = x_ref[:, half:].T
    for g in range(PREPARE_STEPS):
        for copy in inward[g * group : (g + 1) * group]:
            copy.wait()
        outward[g].start()
    for copy in outward:
        copy.wait()


def prepare(x, weights):
    tokens, width = x.shape
    rows, columns = weights.shape
    pieces = columns // width
    half = jax.ShapeDtypeStruct((width // 2, tokens), x.dtype)
    return pl.pallas_call(
        prepare_kernel,
        out_shape=(half, half, jax.ShapeDtypeStruct((pieces, rows, width), weights.dtype)),
        in_specs=[pl.BlockSpec(memory_space=pltpu.VMEM), pl.BlockSpec(memory_space=pl.ANY)],
        out_specs=(
            pl.BlockSpec(memory_space=pltpu.VMEM),
            pl.BlockSpec(memory_space=pltpu.VMEM),
            pl.BlockSpec(memory_space=pl.ANY),
        ),
        scratch_shapes=[
            pltpu.VMEM((pieces, rows, width), weights.dtype),
            pltpu.SemaphoreType.DMA((pieces,)),
            pltpu.SemaphoreType.DMA((PREPARE_STEPS,)),
        ],
        compiler_params=pltpu.CompilerParams(vmem_limit_bytes=GRANT),
    )(x, weights)


def shifted(value, axis, shift):
    side = lax.axis_size(axis)
    return lax.ppermute(value, axis, [(i, (i + shift) % side) for i in range(side)])


FAR_FIRST = (2, 1, -1)


def gather_plane(high, low):
    lines = [tuple(shifted(half, axis, d) for d in FAR_FIRST) for half, axis in ((high, "x"), (low, "y"))]
    lines = lax.optimization_barrier(lines)
    lines = [jnp.stack((half,) + line) for half, line in zip((high, low), lines)]
    ahead = [shifted(line, axis, -1) for line, axis in zip(lines, ("y", "x"))]
    back = [shifted(line, axis, 1) for line, axis in zip(lines, ("y", "x"))]
    ahead = lax.optimization_barrier(ahead)
    far = [shifted(line, axis, -1) for line, axis in zip(ahead, ("y", "x"))]
    return list(zip(lines, far, back, ahead))


def whiten_kernel(*refs):
    first, second = refs[:4], refs[4:8]
    sketch_ref, out_ref, a_ref, d_ref, inv_ref, acc_ref = refs[8:]
    outer = len(first)
    inner, half, _ = first[0].shape
    width = 2 * half
    panels = width // NB
    wide = 2 * NB

    def pair(x, y, upper):
        parts = [first[y][x + d] if upper else second[x + d][y] for d in range(2)]
        return jnp.concatenate(parts, axis=1)

    for c in range(panels // 2):
        lo = c * wide
        top = bottom = None
        for x in range(0, inner, 2):
            for y in range(outer):
                low_part = pair(x, y, False)
                if lo < half:
                    high_part = pair(x, y, True)
                    right = high_part[lo : lo + wide, :]
                    term = dot(high_part[lo:, :], right, NT)
                    top = term if top is None else top + term
                    term = dot(low_part, right, NT)
                else:
                    at = lo - half
                    term = dot(low_part[at:, :], low_part[at : at + wide, :], NT)
                bottom = term if bottom is None else bottom + term
        if lo < half:
            a_ref[2 * c, lo:half, :] = top[:, :NB]
            a_ref[2 * c + 1, lo:half, :] = top[:, NB:]
        from_row = max(lo, half)
        a_ref[2 * c, from_row:, :] = bottom[:, :NB]
        a_ref[2 * c + 1, from_row:, :] = bottom[:, NB:]

    lane = lax.broadcasted_iota(jnp.int32, (NB, NB), 1)
    sub = lax.broadcasted_iota(jnp.int32, (NB, NB), 0)
    diag = lane == sub
    trace = jnp.zeros((NB, NB), F32)
    for c in range(panels):
        trace = trace + jnp.where(diag, a_ref[c, c * NB : (c + 1) * NB, :], 0.0)
    damp = jnp.sum(trace) * (DAMPING / width)
    for c in range(panels):
        block = a_ref[c, c * NB : (c + 1) * NB, :]
        a_ref[c, c * NB : (c + 1) * NB, :] = jnp.where(diag, block + damp, block)

    inv_ref[...] = jnp.zeros_like(inv_ref)
    acc_ref[...] = jnp.zeros_like(acc_ref)
    d_ref[...] = a_ref[0, :NB, :]

    tall_row = lax.broadcasted_iota(jnp.int32, (width, NB), 0)
    tall_lane = lax.broadcasted_iota(jnp.int32, (width, NB), 1)

    def panel_of(p, inv):
        ih, il = split2(inv)
        ph, pm = split2(a_ref[p])
        panel = dot(jnp.concatenate([ph, pm], axis=1), jnp.concatenate([ih, ih], axis=1), NT) + dot(ph, il, NT)
        return jnp.where(tall_row >= tall_lane + p * NB, panel, 0.0)

    def sketch_in(p, both):
        part = sketch_ref[p]
        acc_ref[...] += dot(jnp.concatenate([part, part], axis=1), both, NT)

    def step(p, carry):
        strips = [d_ref[s * STRIP : (s + 1) * STRIP, :] for s in range(NB // STRIP)]
        before = jnp.maximum(p - 1, 0)
        panel = panel_of(before, inv_ref[...])
        hi, lo16 = split2(panel)
        both = jnp.concatenate([hi, lo16], axis=1)
        right = tall_row >= p * NB
        hi_r = jnp.where(right, panel, 0.0).astype(BF16)
        lo_r = jnp.where(right, panel - hi.astype(F32), 0.0).astype(BF16)
        twice = jnp.concatenate([hi_r, hi_r], axis=1)
        for c in range(panels // 2):
            lo = c * wide
            off = dot(both[lo:], twice[lo : lo + wide], NT) + dot(hi[lo:], lo_r[lo : lo + wide], NT)
            a_ref[2 * c, lo:, :] -= off[:, :NB]
            a_ref[2 * c + 1, lo:, :] -= off[:, NB:]
        sketch_in(before, both)
        factor_into(strips, inv_ref)
        nxt = jnp.minimum(p + 1, panels - 1)
        rows_n = pl.ds(pl.multiple_of(nxt * NB, NB), NB)
        near = dot3(a_ref[p, rows_n, :], inv_ref[...], NT)
        d_ref[...] = a_ref[nxt, rows_n, :] - dot3(near, near, NT)
        return carry

    lax.fori_loop(0, panels, step, 0)
    hi, lo16 = split2(panel_of(panels - 1, inv_ref[...]))
    sketch_in(panels - 1, jnp.concatenate([hi, lo16], axis=1))
    out_ref[...] = acc_ref[...].astype(BF16)


def whiten(first, second, sketch_t):
    width = 2 * first[0].shape[1]
    panels, rmax, _ = sketch_t.shape
    return pl.pallas_call(
        whiten_kernel,
        out_shape=jax.ShapeDtypeStruct((rmax, width), BF16),
        in_specs=[pl.BlockSpec(memory_space=pltpu.VMEM)] * 9,
        out_specs=pl.BlockSpec(memory_space=pltpu.VMEM),
        scratch_shapes=[
            pltpu.VMEM((panels, width, NB), F32),
            pltpu.VMEM((NB, NB), F32),
            pltpu.VMEM((NB, NB), F32),
            pltpu.VMEM((rmax, width), F32),
        ],
        compiler_params=pltpu.CompilerParams(vmem_limit_bytes=24 * 1024 * 1024),
    )(*first, *second, sketch_t)


def basis_kernel(rank_ref, w_ref, sk_ref, turned_ref, basis_ref, first_inv, second_inv):
    width = w_ref.shape[0]
    rmax = sk_ref.shape[0]
    rank = rank_ref[0, 0]
    kept = lax.broadcasted_iota(jnp.int32, sk_ref.shape, 0) < rank
    masked = jnp.where(kept, sk_ref[...].astype(F32), 0.0).astype(BF16)
    rows = dot(masked, w_ref[...], NT)
    inner = dot6(rows, rows, NT)
    sub = lax.broadcasted_iota(jnp.int32, (rmax, rmax), 0)
    lane = lax.broadcasted_iota(jnp.int32, (rmax, rmax), 1)
    inner = inner + jnp.where((sub == lane) & (sub >= rank), 1.0, 0.0)
    inv_ref = (first_inv, second_inv)

    def factor(block, p):
        factor_into([block[s * STRIP : (s + 1) * STRIP] for s in range(NB // STRIP)], inv_ref[p])
        return inv_ref[p][...]

    def put(base, p):
        scaled = base * math.sqrt(width)
        turned_ref[p * NB : (p + 1) * NB, :] = scaled.astype(BF16)
        basis_ref[:, p * NB : (p + 1) * NB] = scaled.T.astype(BF16)

    inv = factor(inner[:NB, :NB], 0)
    low = dot6(inner[NB:, :NB], inv, NT)
    rest = inner[NB:, NB:] - dot6(low, low, NT)
    base = dot3(inv, rows[:NB], NN)
    left = rows[NB:] - dot3(low, base, NN)
    put(base, 0)
    put(dot3(factor(rest, 1), left, NN), 1)


def basis_of(rank, tile_block, sketched_t):
    width = tile_block.shape[0]
    rmax = sketched_t.shape[0]
    return pl.pallas_call(
        basis_kernel,
        out_shape=(
            jax.ShapeDtypeStruct((rmax, width), BF16),
            jax.ShapeDtypeStruct((width, rmax), BF16),
        ),
        in_specs=[
            pl.BlockSpec(memory_space=pltpu.SMEM),
            pl.BlockSpec(memory_space=pltpu.VMEM),
            pl.BlockSpec(memory_space=pltpu.VMEM),
        ],
        out_specs=(pl.BlockSpec(memory_space=pltpu.VMEM),) * 2,
        scratch_shapes=[
            pltpu.VMEM((NB, NB), F32),
            pltpu.VMEM((NB, NB), F32),
        ],
        compiler_params=pltpu.CompilerParams(vmem_limit_bytes=24 * 1024 * 1024),
    )(rank, tile_block, sketched_t)


def local(calibration, sketch, weights, tile_ranks):
    width = calibration.shape[1]
    rmax = sketch.shape[1]
    high, low, pieces = prepare(calibration, weights)
    tile_block = lax.all_to_all(pieces, "tile", split_axis=0, concat_axis=0, tiled=True).reshape(width, width)
    first, second = gather_plane(high, low)
    sketch_t = sketch.reshape(width // NB, NB, rmax).transpose(0, 2, 1)
    sketched_t = whiten(first, second, sketch_t)
    turned, basis = basis_of(tile_ranks, tile_block, sketched_t)
    served = lax.all_to_all(basis, "tile", split_axis=0, concat_axis=1, tiled=True)
    coeffs = jnp.dot(turned, tile_block, preferred_element_type=F32) / math.sqrt(width)
    return (served, coeffs.astype(BF16))


def solution(mesh):
    tokens, tiles = mesh.devices.shape
    side = math.isqrt(tokens)
    plane = jax.sharding.Mesh(mesh.devices.reshape(side, side, tiles), ("x", "y", "tile"))
    dp = ("x", "y")
    return jax.shard_map(
        local,
        mesh=plane,
        in_specs=(P(dp, "tile"), P("tile", None), P((*dp, "tile"), None), P(dp, "tile")),
        out_specs=(P((*dp, "tile"), None), P(dp, "tile")),
        check_vma=False,
    )
```

```python
import functools
import math

import jax
import jax.numpy as jnp
from jax import lax
from jax.experimental import pallas as pl
from jax.experimental.pallas import tpu as pltpu
from jax.sharding import PartitionSpec as P

DAMPING = 0.1
NB = 128
STRIP = 8
PREPARE_STEPS = 4
GRANT = 56 * 1024 * 1024
F32 = jnp.float32
BF16 = jnp.bfloat16

NT = (((1,), (1,)), ((), ()))
NN = (((1,), (0,)), ((), ()))


def dot(a, b, dims):
    return lax.dot_general(a, b, dims, preferred_element_type=F32)


def split2(x):
    hi = x.astype(BF16)
    lo = (x - hi.astype(F32)).astype(BF16)
    return hi, lo


def split3(x):
    hi = x.astype(BF16)
    rest = x - hi.astype(F32)
    mid = rest.astype(BF16)
    lo = (rest - mid.astype(F32)).astype(BF16)
    return hi, mid, lo


def dot3(a, b, dims):
    ah, al = split2(a)
    bh, bl = split2(b)
    return dot(ah, bh, dims) + (dot(ah, bl, dims) + dot(al, bh, dims))


def dot6(a, b, dims):
    ah, am, al = split3(a)
    bh, bm, bl = split3(b)
    small = dot(am, bm, dims) + (dot(ah, bl, dims) + dot(al, bh, dims))
    return dot(ah, bh, dims) + ((dot(ah, bm, dims) + dot(am, bh, dims)) + small)


def inverse_factor(rows):
    shape = rows[0].shape
    lane = lax.broadcasted_iota(jnp.int32, shape, 1)
    sub = lax.broadcasted_iota(jnp.int32, shape, 0)
    rows = list(rows)
    out = []

    def columns(strip, base):
        return [jnp.broadcast_to(strip[:, base + k : base + k + 1], shape) for k in range(STRIP)]

    for s in range(len(rows)):
        base = s * STRIP
        strip = rows[s]
        last = s + 1 == len(rows)
        cols = columns(strip, base)
        a = [
            [jnp.broadcast_to(cols[k][i : i + 1, :], shape) if i >= k else None for k in range(STRIP)]
            for i in range(STRIP)
        ]
        own = (lane >= base) & (lane < base + STRIP)
        held = jnp.where(own, jnp.where(lane - base == sub, 1.0, 0.0), strip)
        y = [jnp.broadcast_to(held[k : k + 1, :], shape) for k in range(STRIP)]
        if not last:
            below = columns(rows[s + 1], base)
            near = jnp.where(own, 0.0, rows[s + 1])
        z = []
        low = [[None] * STRIP for _ in range(STRIP)]
        done = jnp.zeros(shape, F32)
        for k in range(STRIP):
            r = pl.reciprocal(a[k][k], approx=True)
            for i in range(k + 1, STRIP):
                low[i][k] = a[i][k] * r
                for j in range(k + 1, i + 1):
                    a[i][j] = a[i][j] - low[i][k] * a[j][k]
            for i in range(k + 1, STRIP):
                y[i] = y[i] - low[i][k] * y[k]
            if not last:
                low_near = below[k] * r
                for j in range(k + 1, STRIP):
                    below[j] = below[j] - low_near * a[j][k]
                near = near - low_near * y[k]
            z.append(y[k] * r)
            done = jnp.where(sub == k, y[k] * lax.rsqrt(a[k][k]), done)
        out.append(jnp.where(lane < base + STRIP, done, 0.0))
        if last:
            break
        rows[s + 1] = near
        for k in range(STRIP - 1, -1, -1):
            for i in range(k):
                z[i] = z[i] - low[k][i] * z[k]
        for t in range(s + 2, len(rows)):
            taken = columns(rows[t], base)
            total = jnp.where(own, 0.0, rows[t])
            for k in range(STRIP - 1, -1, -1):
                total = total - taken[k] * z[k]
            rows[t] = total
    return out


def factor_into(strips, inv_ref):
    for s, rows in enumerate(inverse_factor(strips)):
        inv_ref[s * STRIP : (s + 1) * STRIP, :] = rows


def prepare_kernel(x_ref, w_ref, high_ref, low_ref, pieces_ref, hold_ref, in_sems, out_sems):
    pieces, _, width = hold_ref.shape
    group = pieces // PREPARE_STEPS
    inward = [
        pltpu.make_async_copy(w_ref.at[:, pl.ds(t * width, width)], hold_ref.at[t], in_sems.at[t]) for t in range(pieces)
    ]
    outward = [
        pltpu.make_async_copy(hold_ref.at[pl.ds(g * group, group)], pieces_ref.at[pl.ds(g * group, group)], out_sems.at[g])
        for g in range(PREPARE_STEPS)
    ]
    for copy in inward:
        copy.start()
    half = high_ref.shape[0]
    high_ref[...] = x_ref[:, :half].T
    low_ref[...] = x_ref[:, half:].T
    for g in range(PREPARE_STEPS):
        for copy in inward[g * group : (g + 1) * group]:
            copy.wait()
        outward[g].start()
    for copy in outward:
        copy.wait()


def prepare(x, weights):
    tokens, width = x.shape
    rows, columns = weights.shape
    pieces = columns // width
    half = jax.ShapeDtypeStruct((width // 2, tokens), x.dtype)
    return pl.pallas_call(
        prepare_kernel,
        out_shape=(half, half, jax.ShapeDtypeStruct((pieces, rows, width), weights.dtype)),
        in_specs=[pl.BlockSpec(memory_space=pltpu.VMEM), pl.BlockSpec(memory_space=pl.ANY)],
        out_specs=(
            pl.BlockSpec(memory_space=pltpu.VMEM),
            pl.BlockSpec(memory_space=pltpu.VMEM),
            pl.BlockSpec(memory_space=pl.ANY),
        ),
        scratch_shapes=[
            pltpu.VMEM((pieces, rows, width), weights.dtype),
            pltpu.SemaphoreType.DMA((pieces,)),
            pltpu.SemaphoreType.DMA((PREPARE_STEPS,)),
        ],
        compiler_params=pltpu.CompilerParams(vmem_limit_bytes=GRANT),
    )(x, weights)


def shifted(value, axis, shift):
    side = lax.axis_size(axis)
    return lax.ppermute(value, axis, [(i, (i + shift) % side) for i in range(side)])


FAR_FIRST = (2, 1, -1)


def gather_plane(high, low):
    lines = [tuple(shifted(half, axis, d) for d in FAR_FIRST) for half, axis in ((high, "x"), (low, "y"))]
    lines = lax.optimization_barrier(lines)
    lines = [jnp.stack((half,) + line) for half, line in zip((high, low), lines)]
    ahead = [shifted(line, axis, -1) for line, axis in zip(lines, ("y", "x"))]
    back = [shifted(line, axis, 1) for line, axis in zip(lines, ("y", "x"))]
    ahead = lax.optimization_barrier(ahead)
    far = [shifted(line, axis, -1) for line, axis in zip(ahead, ("y", "x"))]
    return list(zip(lines, far, back, ahead))


def whiten_kernel(*refs):
    first, second = refs[:4], refs[4:8]
    sketch_ref, out_ref, a_ref, d_ref, inv_ref, acc_ref = refs[8:]
    outer = len(first)
    inner, half, _ = first[0].shape
    width = 2 * half
    panels = width // NB
    wide = 2 * NB

    def pair(x, y, upper):
        parts = [first[y][x + d] if upper else second[x + d][y] for d in range(2)]
        return jnp.concatenate(parts, axis=1)

    lane = lax.broadcasted_iota(jnp.int32, (NB, NB), 1)
    sub = lax.broadcasted_iota(jnp.int32, (NB, NB), 0)
    diag = lane == sub

    def gram_columns(c):
        lo = c * wide
        top = bottom = None
        for x in range(0, inner, 2):
            for y in range(outer):
                low_part = pair(x, y, False)
                if lo < half:
                    high_part = pair(x, y, True)
                    right = high_part[lo : lo + wide, :]
                    term = dot(high_part[lo:, :], right, NT)
                    top = term if top is None else top + term
                    term = dot(low_part, right, NT)
                else:
                    at = lo - half
                    term = dot(low_part[at:, :], low_part[at : at + wide, :], NT)
                bottom = term if bottom is None else bottom + term
        if lo < half:
            a_ref[2 * c, lo:half, :] = top[:, :NB]
            a_ref[2 * c + 1, lo:half, :] = top[:, NB:]
        from_row = max(lo, half)
        a_ref[2 * c, from_row:, :] = bottom[:, :NB]
        a_ref[2 * c + 1, from_row:, :] = bottom[:, NB:]

    def square_sum():
        total = jnp.zeros((STRIP, NB), F32)
        for parts in (first, second):
            for part in parts:
                for d in range(inner):
                    values = part[d].astype(F32)
                    total = total + jnp.sum((values * values).reshape(half // STRIP, STRIP, NB), axis=0)
        return jnp.sum(total)

    damp = square_sum() * (DAMPING / width)

    def damped(c):
        block = a_ref[c, c * NB : (c + 1) * NB, :]
        block = jnp.where(diag, block + damp, block)
        a_ref[c, c * NB : (c + 1) * NB, :] = block
        return block

    def strips_of(block):
        return [block[s * STRIP : (s + 1) * STRIP, :] for s in range(NB // STRIP)]

    gram_columns(0)
    block = damped(0)
    for c in range(1, panels // 2):
        gram_columns(c)
    for c in range(1, panels):
        damped(c)
    acc_ref[...] = jnp.zeros_like(acc_ref)
    factor_into(strips_of(block), inv_ref)

    def near_block(p, nxt):
        rows_n = pl.ds(pl.multiple_of(nxt * NB, NB), NB)
        near = dot3(a_ref[p, rows_n, :], inv_ref[...], NT)
        d_ref[...] = a_ref[nxt, rows_n, :] - dot3(near, near, NT)

    near_block(0, 1)

    tall_row = lax.broadcasted_iota(jnp.int32, (width, NB), 0)
    tall_lane = lax.broadcasted_iota(jnp.int32, (width, NB), 1)

    def panel_of(p, inv):
        ih, il = split2(inv)
        ph, pm = split2(a_ref[p])
        panel = dot(jnp.concatenate([ph, pm], axis=1), jnp.concatenate([ih, ih], axis=1), NT) + dot(ph, il, NT)
        return jnp.where(tall_row >= tall_lane + p * NB, panel, 0.0)

    def sketch_of(p):
        part = sketch_ref[pl.ds(pl.multiple_of(p * NB, NB), NB), :].T
        return jnp.concatenate([part, part], axis=1)

    def step(p, carry):
        strips = strips_of(d_ref[...])
        before = p - 1
        panel = panel_of(before, inv_ref[...])
        hi, lo16 = split2(panel)
        both = jnp.concatenate([hi, lo16], axis=1)
        right = tall_row >= p * NB
        hi_r = jnp.where(right, panel, 0.0).astype(BF16)
        lo_r = jnp.where(right, panel - hi.astype(F32), 0.0).astype(BF16)
        twice = jnp.concatenate([hi_r, hi_r], axis=1)
        for c in range(panels // 2):
            lo = c * wide
            off = dot(both[lo:], twice[lo : lo + wide], NT) + dot(hi[lo:], lo_r[lo : lo + wide], NT)
            a_ref[2 * c, lo:, :] -= off[:, :NB]
            a_ref[2 * c + 1, lo:, :] -= off[:, NB:]
        acc_ref[...] += dot(sketch_of(before), both, NT)
        factor_into(strips, inv_ref)
        near_block(p, jnp.minimum(p + 1, panels - 1))
        return carry

    lax.fori_loop(1, panels, step, 0)
    top = width - NB
    corner = dot3(a_ref[panels - 1, top:, :], inv_ref[...], NT)
    hi, lo16 = split2(jnp.where(sub >= lane, corner, 0.0))
    last = dot(sketch_of(panels - 1), jnp.concatenate([hi, lo16], axis=1), NT)
    out_ref[:, :top] = acc_ref[:, :top].astype(BF16)
    out_ref[:, top:] = (acc_ref[:, top:] + last).astype(BF16)


def whiten(first, second, sketch):
    width = 2 * first[0].shape[1]
    panels, rmax = width // NB, sketch.shape[1]
    return pl.pallas_call(
        whiten_kernel,
        out_shape=jax.ShapeDtypeStruct((rmax, width), BF16),
        in_specs=[pl.BlockSpec(memory_space=pltpu.VMEM)] * 9,
        out_specs=pl.BlockSpec(memory_space=pltpu.VMEM),
        scratch_shapes=[
            pltpu.VMEM((panels, width, NB), F32),
            pltpu.VMEM((NB, NB), F32),
            pltpu.VMEM((NB, NB), F32),
            pltpu.VMEM((rmax, width), F32),
        ],
        compiler_params=pltpu.CompilerParams(vmem_limit_bytes=24 * 1024 * 1024),
    )(*first, *second, sketch)


def basis_kernel(rank_ref, w_ref, sk_ref, turned_ref, basis_ref, first_inv, second_inv):
    width = w_ref.shape[0]
    rmax = sk_ref.shape[0]
    rank = rank_ref[0, 0]
    kept = lax.broadcasted_iota(jnp.int32, sk_ref.shape, 0) < rank
    masked = jnp.where(kept, sk_ref[...].astype(F32), 0.0).astype(BF16)
    rows = dot(masked, w_ref[...], NT)
    inner = dot6(rows, rows, NT)
    sub = lax.broadcasted_iota(jnp.int32, (rmax, rmax), 0)
    lane = lax.broadcasted_iota(jnp.int32, (rmax, rmax), 1)
    inner = inner + jnp.where((sub == lane) & (sub >= rank), 1.0, 0.0)
    inv_ref = (first_inv, second_inv)

    def factor(block, p):
        factor_into([block[s * STRIP : (s + 1) * STRIP] for s in range(NB // STRIP)], inv_ref[p])
        return inv_ref[p][...]

    def put(base, p):
        scaled = base * math.sqrt(width)
        turned_ref[p * NB : (p + 1) * NB, :] = scaled.astype(BF16)
        basis_ref[:, p * NB : (p + 1) * NB] = scaled.T.astype(BF16)

    inv = factor(inner[:NB, :NB], 0)
    low = dot6(inner[NB:, :NB], inv, NT)
    rest = inner[NB:, NB:] - dot6(low, low, NT)
    base = dot3(inv, rows[:NB], NN)
    left = rows[NB:] - dot3(low, base, NN)
    put(base, 0)
    put(dot3(factor(rest, 1), left, NN), 1)


def basis_of(rank, tile_block, sketched_t):
    width = tile_block.shape[0]
    rmax = sketched_t.shape[0]
    return pl.pallas_call(
        basis_kernel,
        out_shape=(
            jax.ShapeDtypeStruct((rmax, width), BF16),
            jax.ShapeDtypeStruct((width, rmax), BF16),
        ),
        in_specs=[
            pl.BlockSpec(memory_space=pltpu.SMEM),
            pl.BlockSpec(memory_space=pltpu.VMEM),
            pl.BlockSpec(memory_space=pltpu.VMEM),
        ],
        out_specs=(pl.BlockSpec(memory_space=pltpu.VMEM),) * 2,
        scratch_shapes=[
            pltpu.VMEM((NB, NB), F32),
            pltpu.VMEM((NB, NB), F32),
        ],
        compiler_params=pltpu.CompilerParams(vmem_limit_bytes=24 * 1024 * 1024),
    )(rank, tile_block, sketched_t)


def local(calibration, sketch, weights, tile_ranks):
    width = calibration.shape[1]
    high, low, pieces = prepare(calibration, weights)
    tile_block = lax.all_to_all(pieces, "tile", split_axis=0, concat_axis=0, tiled=True).reshape(width, width)
    first, second = gather_plane(high, low)
    sketched_t = whiten(first, second, sketch)
    turned, basis = basis_of(tile_ranks, tile_block, sketched_t)
    served = lax.all_to_all(basis, "tile", split_axis=0, concat_axis=1, tiled=True)
    coeffs = jnp.dot(turned, tile_block, preferred_element_type=F32) / math.sqrt(width)
    return (served, coeffs.astype(BF16))


def solution(mesh):
    tokens, tiles = mesh.devices.shape
    side = math.isqrt(tokens)
    plane = jax.sharding.Mesh(mesh.devices.reshape(side, side, tiles), ("x", "y", "tile"))
    dp = ("x", "y")
    return jax.shard_map(
        local,
        mesh=plane,
        in_specs=(P(dp, "tile"), P("tile", None), P((*dp, "tile"), None), P(dp, "tile")),
        out_specs=(P((*dp, "tile"), None), P(dp, "tile")),
        check_vma=False,
    )
```

```python
import functools
import math

import jax
import jax.numpy as jnp
from jax import lax
from jax.experimental import pallas as pl
from jax.experimental.pallas import tpu as pltpu
from jax.sharding import PartitionSpec as P

DAMPING = 0.1
NB = 128
STRIP = 8
PREPARE_STEPS = 4
GRANT = 56 * 1024 * 1024
F32 = jnp.float32
BF16 = jnp.bfloat16

NT = (((1,), (1,)), ((), ()))
NN = (((1,), (0,)), ((), ()))


def dot(a, b, dims):
    return lax.dot_general(a, b, dims, preferred_element_type=F32)


def split2(x):
    hi = x.astype(BF16)
    lo = (x - hi.astype(F32)).astype(BF16)
    return hi, lo


def split3(x):
    hi = x.astype(BF16)
    rest = x - hi.astype(F32)
    mid = rest.astype(BF16)
    lo = (rest - mid.astype(F32)).astype(BF16)
    return hi, mid, lo


def dot3(a, b, dims):
    ah, al = split2(a)
    bh, bl = split2(b)
    return dot(ah, bh, dims) + (dot(ah, bl, dims) + dot(al, bh, dims))


def dot6(a, b, dims):
    ah, am, al = split3(a)
    bh, bm, bl = split3(b)
    small = dot(am, bm, dims) + (dot(ah, bl, dims) + dot(al, bh, dims))
    return dot(ah, bh, dims) + ((dot(ah, bm, dims) + dot(am, bh, dims)) + small)


def inverse_factor(rows):
    shape = rows[0].shape
    lane = lax.broadcasted_iota(jnp.int32, shape, 1)
    sub = lax.broadcasted_iota(jnp.int32, shape, 0)
    rows = list(rows)
    out = []

    def columns(strip, base):
        return [jnp.broadcast_to(strip[:, base + k : base + k + 1], shape) for k in range(STRIP)]

    for s in range(len(rows)):
        base = s * STRIP
        strip = rows[s]
        last = s + 1 == len(rows)
        cols = columns(strip, base)
        a = [
            [jnp.broadcast_to(cols[k][i : i + 1, :], shape) if i >= k else None for k in range(STRIP)]
            for i in range(STRIP)
        ]
        own = (lane >= base) & (lane < base + STRIP)
        held = jnp.where(own, jnp.where(lane - base == sub, 1.0, 0.0), strip)
        y = [jnp.broadcast_to(held[k : k + 1, :], shape) for k in range(STRIP)]
        if not last:
            below = columns(rows[s + 1], base)
            near = jnp.where(own, 0.0, rows[s + 1])
        z = []
        low = [[None] * STRIP for _ in range(STRIP)]
        done = jnp.zeros(shape, F32)
        for k in range(STRIP):
            r = pl.reciprocal(a[k][k], approx=True)
            for i in range(k + 1, STRIP):
                low[i][k] = a[i][k] * r
                for j in range(k + 1, i + 1):
                    a[i][j] = a[i][j] - low[i][k] * a[j][k]
            for i in range(k + 1, STRIP):
                y[i] = y[i] - low[i][k] * y[k]
            if not last:
                low_near = below[k] * r
                for j in range(k + 1, STRIP):
                    below[j] = below[j] - low_near * a[j][k]
                near = near - low_near * y[k]
            z.append(y[k] * r)
            done = jnp.where(sub == k, y[k] * lax.rsqrt(a[k][k]), done)
        out.append(jnp.where(lane < base + STRIP, done, 0.0))
        if last:
            break
        rows[s + 1] = near
        for k in range(STRIP - 1, -1, -1):
            for i in range(k):
                z[i] = z[i] - low[k][i] * z[k]
        for t in range(s + 2, len(rows)):
            taken = columns(rows[t], base)
            total = jnp.where(own, 0.0, rows[t])
            for k in range(STRIP - 1, -1, -1):
                total = total - taken[k] * z[k]
            rows[t] = total
    return out


def factor_into(strips, inv_ref):
    for s, rows in enumerate(inverse_factor(strips)):
        inv_ref[s * STRIP : (s + 1) * STRIP, :] = rows


def prepare_kernel(x_ref, w_ref, high_ref, low_ref, pieces_ref, hold_ref, x_hold, turned, in_sems, out_sems, x_sems):
    pieces, _, width = hold_ref.shape
    group = pieces // PREPARE_STEPS
    inward = [
        pltpu.make_async_copy(w_ref.at[:, pl.ds(t * width, width)], hold_ref.at[t], in_sems.at[t]) for t in range(pieces)
    ]
    outward = [
        pltpu.make_async_copy(hold_ref.at[pl.ds(g * group, group)], pieces_ref.at[pl.ds(g * group, group)], out_sems.at[g])
        for g in range(PREPARE_STEPS)
    ]
    load = pltpu.make_async_copy(x_ref, x_hold, x_sems.at[2])
    load.start()
    for copy in inward:
        copy.start()
    load.wait()
    half = high_ref.shape[0]
    stores = []
    for i, ref in enumerate((high_ref, low_ref)):
        turned[i] = x_hold[:, i * half : (i + 1) * half].T
        stores.append(pltpu.make_async_copy(turned.at[i], ref, x_sems.at[i]))
        stores[i].start()
    for g in range(PREPARE_STEPS):
        for copy in inward[g * group : (g + 1) * group]:
            copy.wait()
        outward[g].start()
    for copy in outward + stores:
        copy.wait()


def prepare(x, weights):
    tokens, width = x.shape
    rows, columns = weights.shape
    pieces = columns // width
    half = jax.ShapeDtypeStruct((width // 2, tokens), x.dtype)
    return pl.pallas_call(
        prepare_kernel,
        out_shape=(half, half, jax.ShapeDtypeStruct((pieces, rows, width), weights.dtype)),
        in_specs=[pl.BlockSpec(memory_space=pl.ANY)] * 2,
        out_specs=(pl.BlockSpec(memory_space=pl.ANY),) * 3,
        scratch_shapes=[
            pltpu.VMEM((pieces, rows, width), weights.dtype),
            pltpu.VMEM((tokens, width), x.dtype),
            pltpu.VMEM((2, width // 2, tokens), x.dtype),
            pltpu.SemaphoreType.DMA((pieces,)),
            pltpu.SemaphoreType.DMA((PREPARE_STEPS,)),
            pltpu.SemaphoreType.DMA((3,)),
        ],
        compiler_params=pltpu.CompilerParams(vmem_limit_bytes=GRANT),
    )(x, weights)


def shifted(value, axis, shift):
    side = lax.axis_size(axis)
    return lax.ppermute(value, axis, [(i, (i + shift) % side) for i in range(side)])


FAR_FIRST = (2, 1, -1)


def gather_plane(high, low):
    lines = [tuple(shifted(half, axis, d) for d in FAR_FIRST) for half, axis in ((high, "x"), (low, "y"))]
    lines = lax.optimization_barrier(lines)
    lines = [jnp.stack((half,) + line) for half, line in zip((high, low), lines)]
    ahead = [shifted(line, axis, -1) for line, axis in zip(lines, ("y", "x"))]
    back = [shifted(line, axis, 1) for line, axis in zip(lines, ("y", "x"))]
    ahead = lax.optimization_barrier(ahead)
    far = [shifted(line, axis, -1) for line, axis in zip(ahead, ("y", "x"))]
    return list(zip(lines, far, back, ahead))


def whiten_kernel(*refs):
    first, second = refs[:4], refs[4:8]
    sketch_ref, out_ref, a_ref, d_ref, inv_ref, acc_ref = refs[8:]
    outer = len(first)
    inner, half, _ = first[0].shape
    width = 2 * half
    panels = width // NB
    wide = 2 * NB

    def pair(x, y, upper):
        parts = [first[y][x + d] if upper else second[x + d][y] for d in range(2)]
        return jnp.concatenate(parts, axis=1)

    lane = lax.broadcasted_iota(jnp.int32, (NB, NB), 1)
    sub = lax.broadcasted_iota(jnp.int32, (NB, NB), 0)
    diag = lane == sub

    def gram_columns(c):
        lo = c * wide
        top = bottom = None
        for x in range(0, inner, 2):
            for y in range(outer):
                low_part = pair(x, y, False)
                if lo < half:
                    high_part = pair(x, y, True)
                    right = high_part[lo : lo + wide, :]
                    term = dot(high_part[lo:, :], right, NT)
                    top = term if top is None else top + term
                    term = dot(low_part, right, NT)
                else:
                    at = lo - half
                    term = dot(low_part[at:, :], low_part[at : at + wide, :], NT)
                bottom = term if bottom is None else bottom + term
        if lo < half:
            a_ref[2 * c, lo:half, :] = top[:, :NB]
            a_ref[2 * c + 1, lo:half, :] = top[:, NB:]
        from_row = max(lo, half)
        a_ref[2 * c, from_row:, :] = bottom[:, :NB]
        a_ref[2 * c + 1, from_row:, :] = bottom[:, NB:]

    def square_sum():
        total = jnp.zeros((STRIP, NB), F32)
        for parts in (first, second):
            for part in parts:
                for d in range(inner):
                    values = part[d].astype(F32)
                    total = total + jnp.sum((values * values).reshape(half // STRIP, STRIP, NB), axis=0)
        return jnp.sum(total)

    damp = square_sum() * (DAMPING / width)

    def damped(c):
        block = a_ref[c, c * NB : (c + 1) * NB, :]
        block = jnp.where(diag, block + damp, block)
        a_ref[c, c * NB : (c + 1) * NB, :] = block
        return block

    def strips_of(block):
        return [block[s * STRIP : (s + 1) * STRIP, :] for s in range(NB // STRIP)]

    gram_columns(0)
    block = damped(0)
    for c in range(1, panels // 2):
        gram_columns(c)
    for c in range(1, panels):
        damped(c)
    acc_ref[...] = jnp.zeros_like(acc_ref)
    factor_into(strips_of(block), inv_ref)

    def near_block(p, nxt):
        rows_n = pl.ds(pl.multiple_of(nxt * NB, NB), NB)
        near = dot3(a_ref[p, rows_n, :], inv_ref[...], NT)
        d_ref[...] = a_ref[nxt, rows_n, :] - dot3(near, near, NT)

    near_block(0, 1)

    tall_row = lax.broadcasted_iota(jnp.int32, (width, NB), 0)
    tall_lane = lax.broadcasted_iota(jnp.int32, (width, NB), 1)

    def panel_of(p, inv):
        ih, il = split2(inv)
        ph, pm = split2(a_ref[p])
        panel = dot(jnp.concatenate([ph, pm], axis=1), jnp.concatenate([ih, ih], axis=1), NT) + dot(ph, il, NT)
        return jnp.where(tall_row >= tall_lane + p * NB, panel, 0.0)

    def sketch_of(p):
        part = sketch_ref[pl.ds(pl.multiple_of(p * NB, NB), NB), :].T
        return jnp.concatenate([part, part], axis=1)

    def step(p, carry):
        strips = strips_of(d_ref[...])
        before = p - 1
        panel = panel_of(before, inv_ref[...])
        hi, lo16 = split2(panel)
        both = jnp.concatenate([hi, lo16], axis=1)
        right = tall_row >= p * NB
        hi_r = jnp.where(right, panel, 0.0).astype(BF16)
        lo_r = jnp.where(right, panel - hi.astype(F32), 0.0).astype(BF16)
        twice = jnp.concatenate([hi_r, hi_r], axis=1)
        for c in range(panels // 2):
            lo = c * wide
            off = dot(both[lo:], twice[lo : lo + wide], NT) + dot(hi[lo:], lo_r[lo : lo + wide], NT)
            a_ref[2 * c, lo:, :] -= off[:, :NB]
            a_ref[2 * c + 1, lo:, :] -= off[:, NB:]
        acc_ref[...] += dot(sketch_of(before), both, NT)
        factor_into(strips, inv_ref)
        near_block(p, jnp.minimum(p + 1, panels - 1))
        return carry

    lax.fori_loop(1, panels, step, 0)
    top = width - NB
    corner = dot3(a_ref[panels - 1, top:, :], inv_ref[...], NT)
    hi, lo16 = split2(jnp.where(sub >= lane, corner, 0.0))
    last = dot(sketch_of(panels - 1), jnp.concatenate([hi, lo16], axis=1), NT)
    out_ref[:, :top] = acc_ref[:, :top].astype(BF16)
    out_ref[:, top:] = (acc_ref[:, top:] + last).astype(BF16)


def whiten(first, second, sketch):
    width = 2 * first[0].shape[1]
    panels, rmax = width // NB, sketch.shape[1]
    return pl.pallas_call(
        whiten_kernel,
        out_shape=jax.ShapeDtypeStruct((rmax, width), BF16),
        in_specs=[pl.BlockSpec(memory_space=pltpu.VMEM)] * 9,
        out_specs=pl.BlockSpec(memory_space=pltpu.VMEM),
        scratch_shapes=[
            pltpu.VMEM((panels, width, NB), F32),
            pltpu.VMEM((NB, NB), F32),
            pltpu.VMEM((NB, NB), F32),
            pltpu.VMEM((rmax, width), F32),
        ],
        compiler_params=pltpu.CompilerParams(vmem_limit_bytes=24 * 1024 * 1024),
    )(*first, *second, sketch)


def basis_kernel(rank_ref, w_ref, sk_ref, turned_ref, basis_ref, first_inv, second_inv):
    width = w_ref.shape[0]
    rmax = sk_ref.shape[0]
    rank = rank_ref[0, 0]
    kept = lax.broadcasted_iota(jnp.int32, sk_ref.shape, 0) < rank
    masked = jnp.where(kept, sk_ref[...].astype(F32), 0.0).astype(BF16)
    rows = dot(masked, w_ref[...], NT)
    inner = dot6(rows, rows, NT)
    sub = lax.broadcasted_iota(jnp.int32, (rmax, rmax), 0)
    lane = lax.broadcasted_iota(jnp.int32, (rmax, rmax), 1)
    inner = inner + jnp.where((sub == lane) & (sub >= rank), 1.0, 0.0)
    inv_ref = (first_inv, second_inv)

    def factor(block, p):
        factor_into([block[s * STRIP : (s + 1) * STRIP] for s in range(NB // STRIP)], inv_ref[p])
        return inv_ref[p][...]

    def put(base, p):
        scaled = base * math.sqrt(width)
        turned_ref[p * NB : (p + 1) * NB, :] = scaled.astype(BF16)
        basis_ref[:, p * NB : (p + 1) * NB] = scaled.T.astype(BF16)

    inv = factor(inner[:NB, :NB], 0)
    low = dot6(inner[NB:, :NB], inv, NT)
    rest = inner[NB:, NB:] - dot6(low, low, NT)
    base = dot3(inv, rows[:NB], NN)
    left = rows[NB:] - dot3(low, base, NN)
    put(base, 0)
    put(dot3(factor(rest, 1), left, NN), 1)


def basis_of(rank, tile_block, sketched_t):
    width = tile_block.shape[0]
    rmax = sketched_t.shape[0]
    return pl.pallas_call(
        basis_kernel,
        out_shape=(
            jax.ShapeDtypeStruct((rmax, width), BF16),
            jax.ShapeDtypeStruct((width, rmax), BF16),
        ),
        in_specs=[
            pl.BlockSpec(memory_space=pltpu.SMEM),
            pl.BlockSpec(memory_space=pltpu.VMEM),
            pl.BlockSpec(memory_space=pltpu.VMEM),
        ],
        out_specs=(pl.BlockSpec(memory_space=pltpu.VMEM),) * 2,
        scratch_shapes=[
            pltpu.VMEM((NB, NB), F32),
            pltpu.VMEM((NB, NB), F32),
        ],
        compiler_params=pltpu.CompilerParams(vmem_limit_bytes=24 * 1024 * 1024),
    )(rank, tile_block, sketched_t)


def local(calibration, sketch, weights, tile_ranks):
    width = calibration.shape[1]
    high, low, pieces = prepare(calibration, weights)
    tile_block = lax.all_to_all(pieces, "tile", split_axis=0, concat_axis=0, tiled=True).reshape(width, width)
    first, second = gather_plane(high, low)
    sketched_t = whiten(first, second, sketch)
    turned, basis = basis_of(tile_ranks, tile_block, sketched_t)
    served = lax.all_to_all(basis, "tile", split_axis=0, concat_axis=1, tiled=True)
    coeffs = jnp.dot(turned, tile_block, preferred_element_type=F32) / math.sqrt(width)
    return (served, coeffs.astype(BF16))


def solution(mesh):
    tokens, tiles = mesh.devices.shape
    side = math.isqrt(tokens)
    plane = jax.sharding.Mesh(mesh.devices.reshape(side, side, tiles), ("x", "y", "tile"))
    dp = ("x", "y")
    return jax.shard_map(
        local,
        mesh=plane,
        in_specs=(P(dp, "tile"), P("tile", None), P((*dp, "tile"), None), P(dp, "tile")),
        out_specs=(P((*dp, "tile"), None), P(dp, "tile")),
        check_vma=False,
    )
```
